1024 devices in a mesh: pp: 32 (over y, z_lo), ep: 32 (over x, z_hi, core).
Axes of the slice: x: 4, y: 4, z: 32 (z_hi: 4, z_lo: 8; z = z_hi * 8 + z_lo), core: 2. Of those that a mesh axis runs over, the one named last changes fastest.
Arguments:
- fwd_in: bfloat16 [32, 2048, 3584], P('pp', 'ep'), may hold values from -6 to 6
- fwd_route: int32 [32, 2048, 1], P('pp', 'ep'), may hold values from 0 to 8, as said below
- fwd_gate: float32 [32, 2048, 1], P('pp', 'ep'), may hold values from 0.25 to 1.5
- bwd_cot: bfloat16 [32, 2048, 3584], P('pp', 'ep'), may hold values from -6 to 6
- bwd_route: int32 [32, 2048, 1], P('pp', 'ep'), may hold values from 0 to 8, as said below
- bwd_gate: float32 [32, 2048, 1], P('pp', 'ep'), may hold values from 0.25 to 1.5
- saved_pre: bfloat16 [32, 32, 128, 512], P('pp', 'ep'), may hold values from -6 to 6
- w_gate_up: bfloat16 [32, 3584, 512], P('ep'), may hold values from -0.09375 to 0.09375
- w_down: bfloat16 [32, 256, 3584], P('ep'), may hold values from -0.1875 to 0.1875
Outputs:
- fwd_next: bfloat16 [32, 2048, 3584], P('pp', 'ep')
- bwd_prev: bfloat16 [32, 2048, 3584], P('pp', 'ep')
The draws below stay inside these ranges and needn't reach their ends.
Inputs may be any that keep to these rules, and one draw needn't show every extreme that they name: `fwd_route`: in each section, among the 64 tokens of one index of ep, every expert is named by 1 to 4 tokens and one expert by exactly 4; the other tokens hold 8. `bwd_route`: in each section, among the 64 tokens of one index of ep, every expert is named by 1 to 4 tokens and one expert by exactly 4; the other tokens hold 8.
All inputs are finite; a program needn't handle non-finite values.
Results may differ from the reference program's by a relative error of at most 0.008.
Values may be sent and summed in bfloat16 or wider, within the bound.
No kernel may reach another device: no remote copies, remote signals or barrier semaphores. Data moves between devices by JAX's collectives and lax.ppermute only.
A program may use at most 32 MiB of HBM per device.

```python
import math
import jax
import jax.numpy as jnp
from jax import lax

DW = 3584
FFW = 1024
TOPK = 1
CAP = 4
TOK_DEV = 64
SECTIONS = 32
TOKENS = 2048
SPLIT = 4
HID_DEV = 256
EXPERTS = 8
N_EP = 32


def route_table(key):
    key_count, key_full, key_order = jax.random.split(key, 3)
    counts = jax.random.randint(key_count, (SECTIONS, N_EP, EXPERTS), 1, CAP + 1)
    full = jax.random.randint(key_full, (SECTIONS, N_EP, 1), 0, EXPERTS)
    counts = jnp.where(jnp.arange(EXPERTS, dtype=jnp.int32)[None, None, :] == full, CAP, counts)
    bounds = jnp.cumsum(counts, axis=2)
    scores = jax.random.randint(key_order, (SECTIONS, N_EP, TOK_DEV), 0, 1 << 20) * TOK_DEV + jnp.arange(TOK_DEV, dtype=jnp.int32)[None, None, :]
    order = jnp.argsort(scores, axis=2, stable=True)
    rank = jnp.argsort(order, axis=2, stable=True)
    expert = jnp.sum((rank[..., None] >= bounds[:, :, None, :]).astype(jnp.int32), axis=3)
    return expert.reshape(SECTIONS, TOKENS, 1).astype(jnp.int32)


def draw_fwd_route(key, part):
    key = jax.random.fold_in(key, 11)
    return route_table(key)


def draw_bwd_route(key, part):
    key = jax.random.fold_in(key, 12)
    return route_table(key)


def block_levels(rng, dims, cuts, low, high):
    def one(axis_at, parts):
        heights = jax.random.uniform(jax.random.fold_in(jax.random.fold_in(rng, 6), axis_at), (parts,), jnp.float32, low / len(cuts), high / len(cuts))
        return jnp.repeat(jnp.exp(heights), dims[axis_at] // parts).reshape((-1,) + (1,) * (len(dims) - axis_at - 1))

    factor_of = one(*cuts[0])
    for cut in cuts[1:]:
        factor_of = factor_of * one(*cut)
    return factor_of


def bell_draw(stream_key, dims, scale, limit, cuts=(), kind=jnp.bfloat16):
    result = scale * jax.random.normal(stream_key, dims, jnp.float32)
    if cuts:
        result = result * block_levels(stream_key, dims, cuts, -0.22, 0.18)
    return jnp.clip(result, -limit, limit).astype(kind)


def setup_inputs(seed: int = 0) -> dict:
    seeds = jax.random.split(jax.random.key(seed), 10)
    fwd_in = bell_draw(seeds[0], (SECTIONS, TOKENS, DW), 1.0, 6.0, ((0, 32), (1, 32)))
    fwd_route = draw_fwd_route(jax.random.fold_in(seeds[9], 71), 0)
    fwd_gate = jnp.clip(jnp.exp(math.log(1.5) - 1.7917595 * jax.random.uniform(seeds[2], (SECTIONS, TOKENS, TOPK), jnp.float32) ** block_levels(seeds[2], (SECTIONS, TOKENS, TOPK), ((0, 32), (1, 32)), -0.2, 0.2)), 0.25, 1.5)
    bwd_cot = bell_draw(seeds[3], (SECTIONS, TOKENS, DW), 1.0, 6.0, ((0, 32), (1, 32)))
    bwd_route = draw_bwd_route(jax.random.fold_in(seeds[9], 71), 0)
    bwd_gate = jnp.clip(jnp.exp(math.log(1.5) - 1.7917595 * jax.random.uniform(seeds[5], (SECTIONS, TOKENS, TOPK), jnp.float32) ** block_levels(seeds[5], (SECTIONS, TOKENS, TOPK), ((0, 32), (1, 32)), -0.2, 0.2)), 0.25, 1.5)
    saved_pre = bell_draw(seeds[6], (SECTIONS, N_EP, N_EP * CAP, 2 * HID_DEV), 1.0, 6.0, ((0, 32), (1, 32)))
    w_gate_up = bell_draw(seeds[7], (N_EP, DW, 2 * HID_DEV), DW ** -0.5, 0.09375, ((0, 32),))
    w_down = bell_draw(seeds[8], (N_EP, HID_DEV, DW), FFW ** -0.5, 0.1875, ((0, 32),))
    return {"fwd_in": fwd_in, "fwd_route": fwd_route, "fwd_gate": fwd_gate, "bwd_cot": bwd_cot, "bwd_route": bwd_route, "bwd_gate": bwd_gate, "saved_pre": saved_pre, "w_gate_up": w_gate_up, "w_down": w_down}


def reference(fwd_in, fwd_route, fwd_gate, bwd_cot, bwd_route, bwd_gate, saved_pre, w_gate_up, w_down):
    rows_e = N_EP * CAP
    high = lax.Precision.HIGHEST
    wgu4 = w_gate_up.reshape(EXPERTS, SPLIT, DW, 2 * HID_DEV).astype(jnp.float32)
    wdn4 = w_down.reshape(EXPERTS, SPLIT, HID_DEV, DW).astype(jnp.float32)

    def positions(route):
        source = jnp.arange(TOKENS, dtype=jnp.int32) // TOK_DEV
        onehot = (route[:, None] == jnp.arange(EXPERTS, dtype=jnp.int32)[None, :]).astype(jnp.int32)
        onehot = onehot.reshape(N_EP, TOK_DEV, EXPERTS)
        before = jnp.cumsum(onehot, axis=1) - onehot
        slot = jnp.sum(before * onehot, axis=2).reshape(TOKENS)
        routed = route < EXPERTS
        pos = (route * rows_e + source * CAP + slot).astype(jnp.int32)
        return jnp.where(routed, pos, EXPERTS * rows_e).astype(jnp.int32), routed

    def spread(rows, pos):
        buffer = jnp.zeros((EXPERTS * rows_e + 1, DW), jnp.bfloat16).at[pos].set(rows)
        return buffer[: EXPERTS * rows_e].reshape(EXPERTS, rows_e, DW).astype(jnp.float32)

    def pick(summed, pos):
        padded = jnp.concatenate([summed, jnp.zeros((1, DW), jnp.float32)], axis=0)
        return padded[pos]

    def section(items):
        x_rows, route_f, gate_f, cot, route_b, gate_b, saved = items
        pos_f, routed_f = positions(route_f[:, 0])
        pre = jnp.einsum("grd,gjdh->gjrh", spread(x_rows, pos_f), wgu4, precision=high)
        hidden = (jax.nn.silu(pre[..., :HID_DEV]) * pre[..., HID_DEV:]).astype(jnp.bfloat16)
        part = jnp.einsum("gjrh,gjhd->gjrd", hidden.astype(jnp.float32), wdn4, precision=high).astype(jnp.bfloat16)
        summed = jnp.sum(part.astype(jnp.float32), axis=1).reshape(EXPERTS * rows_e, DW)
        term_f = jnp.where(routed_f[:, None], gate_f * pick(summed, pos_f), 0.0)
        out_rows = (x_rows.astype(jnp.float32) + term_f).astype(jnp.bfloat16)
        pos_b, routed_b = positions(route_b[:, 0])
        scaled = (gate_b * cot.astype(jnp.float32)).astype(jnp.bfloat16)
        dh = jnp.einsum("grd,gjhd->gjrh", spread(scaled, pos_b), wdn4, precision=high)
        saved4 = saved.reshape(EXPERTS, SPLIT, rows_e, 2 * HID_DEV).astype(jnp.float32)
        act = saved4[..., :HID_DEV]
        lin = saved4[..., HID_DEV:]
        sig = jax.nn.sigmoid(act)
        d_act = (dh * lin * sig * (1.0 + act * (1.0 - sig))).astype(jnp.bfloat16)
        d_lin = (dh * act * sig).astype(jnp.bfloat16)
        grads = jnp.concatenate([d_act, d_lin], axis=-1).astype(jnp.float32)
        back = jnp.einsum("gjrh,gjdh->gjrd", grads, wgu4, precision=high).astype(jnp.bfloat16)
        back_sum = jnp.sum(back.astype(jnp.float32), axis=1).reshape(EXPERTS * rows_e, DW)
        term_b = jnp.where(routed_b[:, None], pick(back_sum, pos_b), 0.0)
        grad_rows = (cot.astype(jnp.float32) + term_b).astype(jnp.bfloat16)
        return out_rows, grad_rows

    outputs, gradients = lax.map(section, (fwd_in, fwd_route, fwd_gate, bwd_cot, bwd_route, bwd_gate, saved_pre))
    return jnp.roll(outputs, 1, axis=0), jnp.roll(gradients, -1, axis=0)
```

```python
import jax
import jax.numpy as jnp
from jax import lax
from jax.experimental import pallas as pl
from jax.experimental.pallas import tpu as pltpu
from jax.sharding import Mesh
from jax.sharding import PartitionSpec as P

CORES = 2
Z_GROUPS = 4
SPLIT = 4
F32 = jnp.float32
BF16 = jnp.bfloat16
VMEM = pl.BlockSpec(memory_space=pltpu.VMEM)
SMEM = pl.BlockSpec(memory_space=pltpu.SMEM)
PARAMS = pltpu.CompilerParams(vmem_limit_bytes=44 * 1024 * 1024)


def iota(shape, axis):
    return lax.broadcasted_iota(jnp.int32, shape, axis)


def dot(a, b, dims=((1,), (0,))):
    return lax.dot_general(a, b, (dims, ((), ())), preferred_element_type=F32)


def slots_of(route, experts):
    tokens = route.shape[1]
    onehot = iota((experts, tokens), 0) == route
    onehot = jnp.where(onehot, 1.0, 0.0)
    shape = (tokens, tokens)
    earlier = jnp.where(iota(shape, 0) < iota(shape, 1), 1.0, 0.0).astype(BF16)
    before = dot(onehot.astype(BF16), earlier)
    return jnp.sum(before * onehot, axis=0, keepdims=True)


def column(row):
    tokens = row.shape[1]
    shape = (tokens, tokens)
    on = iota(shape, 0) == iota(shape, 1)
    return jnp.sum(jnp.where(on, row, 0.0), axis=1, keepdims=True)


def pack_kernel(experts, cap, x_ref, rf_ref, cot_ref, rb_ref, gb_ref, out_ref):
    tokens = x_ref.shape[0]
    rows = out_ref.shape[0]
    scaled = (column(gb_ref[...]) * cot_ref[...].astype(F32)).astype(BF16)
    total = jnp.zeros(out_ref.shape, F32)
    for kind, (route, values) in enumerate(((rf_ref[...], x_ref[...]), (rb_ref[...], scaled))):
        slot = slots_of(route, experts).astype(jnp.int32)
        m = iota((rows, tokens), 0)
        table = (m // (4 * cap) == route) & ((m % (2 * cap)) // cap == kind) & (m % cap == slot)
        total += dot(jnp.where(table, 1.0, 0.0).astype(BF16), values)
    out_ref[...] = total.astype(BF16)


def expert_kernel(cap, c_ref, own_ref, oth_ref, saved_ref, wgu_ref, wd_ref, mine_ref, send_ref):
    rows = own_ref.shape[0]
    hid, width = wd_ref.shape
    values = jnp.concatenate([own_ref[...], oth_ref[...]], axis=0)
    both = 2 * rows
    pre = dot(values, wgu_ref[...])
    gate = pre[:, :hid]
    hidden = (gate / (1.0 + jnp.exp(-gate)) * pre[:, hid:]).astype(BF16)
    dh = dot(values, wd_ref[...], ((1,), (1,)))
    r = iota((both, rows), 0)
    p = iota((both, rows), 1)
    core = jnp.where(r < rows, c_ref[0], 1 - c_ref[0])
    r = r % rows
    pick = (p // (2 * cap) == r // (2 * cap)) & (p % cap == r % cap) & ((p % (2 * cap)) // cap == core)
    saved = dot(jnp.where(pick, 1.0, 0.0).astype(BF16), saved_ref[...])
    act = saved[:, :hid]
    lin = saved[:, hid:]
    sig = 1.0 / (1.0 + jnp.exp(-act))
    d_act = (dh * lin * sig * (1.0 + act * (1.0 - sig))).astype(BF16)
    d_lin = (dh * act * sig).astype(BF16)
    zero = jnp.zeros((), BF16)
    forward = (iota((both, hid), 0) % (2 * cap)) // cap == 0
    hidden = jnp.where(forward, hidden, zero)
    grads = jnp.concatenate(
        [jnp.where(forward, zero, d_act), jnp.where(forward, zero, d_lin)], axis=1
    )
    step = 512 if width % 512 == 0 else width
    for at in range(0, width, step):
        part = dot(hidden, wd_ref[:, at : at + step])
        part += dot(grads, wgu_ref[at : at + step, :], ((1,), (1,)))
        part = part.astype(BF16)
        mine_ref[:, at : at + step] = part[:rows]
        send_ref[:, at : at + step] = part[rows:]


def final_kernel(experts, cap, x_ref, rf_ref, gf_ref, cot_ref, rb_ref, back_ref, f_ref, b_ref):
    tokens = x_ref.shape[0]
    rows = back_ref.shape[0]
    back = back_ref[...]
    sums = []
    for kind, route in enumerate((rf_ref[...], rb_ref[...])):
        slot = column(slots_of(route, experts)).astype(jnp.int32)
        expert = column(route.astype(F32)).astype(jnp.int32)
        m = iota((tokens, rows), 1)
        table = (m // (4 * cap) == expert) & ((m % (2 * cap)) // cap == kind) & (m % cap == slot)
        sums.append(dot(jnp.where(table, 1.0, 0.0).astype(BF16), back))
    f_ref[...] = (x_ref[...].astype(F32) + column(gf_ref[...]) * sums[0]).astype(BF16)
    b_ref[...] = (cot_ref[...].astype(F32) + sums[1]).astype(BF16)


def call(kernel, out, operands, flops):
    nbytes = sum(a.size * a.dtype.itemsize for a in (*operands, *out))
    scalar = [a.ndim == 1 for a in operands]
    return pl.pallas_call(
        kernel,
        out_shape=out,
        in_specs=[SMEM if s else VMEM for s in scalar],
        out_specs=[VMEM] * len(out),
        compiler_params=PARAMS,
        cost_estimate=pl.CostEstimate(flops=flops, bytes_accessed=nbytes, transcendentals=0),
    )(*operands)


def swap_core(block):
    return lax.ppermute(block, "c", [(0, 1), (1, 0)])


def shift(block, distance):
    count = lax.axis_size("pp")
    return lax.ppermute(block, "pp", [(i, (i + distance) % count) for i in range(count)])


def exchange(rows, cap):
    width = rows.shape[1]
    blocks = rows.reshape(-1, 2 * cap, width)
    blocks = lax.all_to_all(blocks, ("x", "zh"), split_axis=0, concat_axis=0, tiled=True)
    return blocks.reshape(-1, width)


def shards(fwd_in, fwd_route, fwd_gate, bwd_cot, bwd_route, bwd_gate, saved_pre, w_gate_up, w_down):
    devices = lax.axis_size(("x", "zh", "c"))
    experts = devices // SPLIT
    cap = saved_pre.shape[2] // devices
    x = fwd_in[0]
    cot = bwd_cot[0]
    tokens, width = x.shape
    hid = w_down.shape[1]
    route_f, gate_f, route_b, gate_b = (
        a.reshape(1, tokens) for a in (fwd_route, fwd_gate, bwd_route, bwd_gate)
    )
    rows = devices * cap
    slab = jax.ShapeDtypeStruct((rows, width), BF16)
    out = jax.ShapeDtypeStruct((tokens, width), BF16)
    core = lax.axis_index("c").astype(jnp.int32).reshape(1)

    def pack(*refs):
        pack_kernel(experts, cap, *refs)

    def expert(*refs):
        expert_kernel(cap, *refs)

    def final(*refs):
        final_kernel(experts, cap, *refs)

    (packed,) = call(pack, [slab], (x, route_f, cot, route_b, gate_b), 2 * rows * tokens * width * 2)
    own = exchange(packed, cap)
    other = swap_core(own)
    mine, send = call(
        expert,
        [slab, slab],
        (core, own, other, saved_pre[0, 0], w_gate_up[0], w_down[0]),
        12 * rows * hid * width,
    )
    taken = swap_core(send)
    summed = (mine.astype(F32) + taken.astype(F32)).astype(BF16)
    back = exchange(summed, cap)
    out_f, out_b = call(
        final, [out, out], (x, route_f, gate_f, cot, route_b, back), 4 * rows * tokens * width
    )
    return shift(out_f[None], 1), shift(out_b[None], -1)


def solution(mesh):
    sections, members = mesh.devices.shape
    fine = Mesh(
        mesh.devices.reshape(sections, members // (Z_GROUPS * CORES), Z_GROUPS, CORES),
        ("pp", "x", "zh", "c"),
    )
    ep = ("x", "zh", "c")
    rows = P("pp", ep, None)
    return jax.shard_map(
        shards,
        mesh=fine,
        in_specs=(rows,) * 6 + (P("pp", ep, None, None), P(ep, None, None), P(ep, None, None)),
        out_specs=(rows, rows),
        check_vma=False,
    )
```

```python
import jax
import jax.numpy as jnp
from jax import lax
from jax.experimental import pallas as pl
from jax.experimental.pallas import tpu as pltpu
from jax.sharding import Mesh
from jax.sharding import PartitionSpec as P

CORES = 2
Z_GROUPS = 4
SPLIT = 4
HIDES = {"pack_b": 1e11, "join_b":1e11, "merge_b":1e11,"expert_f":1e11,"pack_f":1e10}
F32 = jnp.float32
BF16 = jnp.bfloat16
VMEM = pl.BlockSpec(memory_space=pltpu.VMEM)
ANY = pl.BlockSpec(memory_space=pl.ANY)
SMEM = pl.BlockSpec(memory_space=pltpu.SMEM)
PARAMS = pltpu.CompilerParams(vmem_limit_bytes=44 * 1024 * 1024)


def iota(shape, axis):
    return lax.broadcasted_iota(jnp.int32, shape, axis)


def dot(a, b, dims=((1,), (0,))):
    return lax.dot_general(a, b, (dims, ((), ())), preferred_element_type=F32)


def ones_at(where):
    return jnp.where(where, 1.0, 0.0).astype(BF16)


def slots_of(route, experts):
    tokens = route.shape[1]
    onehot = jnp.where(iota((experts, tokens), 0) == route, 1.0, 0.0)
    shape = (tokens, tokens)
    before = dot(onehot.astype(BF16), ones_at(iota(shape, 0) < iota(shape, 1)))
    return jnp.sum(before * onehot, axis=0, keepdims=True).astype(jnp.int32)


def column(row):
    tokens = row.shape[1]
    shape = (tokens, tokens)
    on = iota(shape, 0) == iota(shape, 1)
    return jnp.sum(jnp.where(on, row, jnp.zeros((), row.dtype)), axis=1, keepdims=True)


def pack_b_kernel(experts, cap, at_ref, cot_ref, route_ref, gate_ref, *out_refs):
    tokens = cot_ref.shape[0]
    scaled = (column(gate_ref[...]) * cot_ref[...].astype(F32)).astype(BF16)
    route = route_ref[...]
    slot = slots_of(route, experts)
    count = len(out_refs)
    m = iota((count * 2 * cap, tokens), 0)
    pair = at_ref[1] // 2 ^ ((m % (2 * cap)) // cap)
    expert = (at_ref[0] + m // (2 * cap)) % count * 2 + pair
    packed = dot(ones_at((expert == route) & (m % cap == slot)), scaled).astype(BF16)
    for d, out_ref in enumerate(out_refs):
        out_ref[...] = packed[d * 2 * cap : (d + 1) * 2 * cap]


def pairs_kernel(cap, *refs):
    *in_refs, own_ref, oth_ref = refs
    rows = jnp.concatenate([r[...] for r in in_refs], axis=0)
    shape = (own_ref.shape[0], rows.shape[0])
    r, m = iota(shape, 0), iota(shape, 1)
    same = (m // (2 * cap) == r // cap) & (m % cap == r % cap)
    own = (m % (2 * cap)) // cap == 0
    own_ref[...] = dot(ones_at(same & own), rows).astype(BF16)
    oth_ref[...] = dot(ones_at(same & ~own), rows).astype(BF16)


def expert_b_kernel(cap, at_ref, own_ref, oth_ref, saved_ref, wgu_ref, wd_ref, mine_ref, send_ref):
    rows = own_ref.shape[0]
    hid, width = wd_ref.shape
    values = jnp.concatenate([own_ref[...], oth_ref[...]], axis=0)
    dh = dot(values, wd_ref[...], ((1,), (1,)))
    shape = (2 * rows, saved_ref.shape[0])
    r, p = iota(shape, 0), iota(shape, 1)
    core = at_ref[2] ^ (r // rows)
    block = (r % rows) // (rows // Z_GROUPS)
    mask = block ^ (block // 2)
    count = rows // (Z_GROUPS * cap)
    source_x = (at_ref[0] + count - (r // cap) % count) % count
    source = (source_x * Z_GROUPS + (at_ref[1] ^ mask)) * CORES + core
    saved = dot(ones_at(p == source * cap + r % cap), saved_ref[...])
    act = saved[:, :hid]
    lin = saved[:, hid:]
    sig = 1.0 / (1.0 + jnp.exp(-act))
    d_act = (dh * lin * sig * (1.0 + act * (1.0 - sig))).astype(BF16)
    d_lin = (dh * act * sig).astype(BF16)
    grads = jnp.concatenate([d_act, d_lin], axis=1)
    step = 512 if width % 512 == 0 else width
    for at in range(0, width, step):
        part = dot(grads, wgu_ref[at : at + step, :], ((1,), (1,))).astype(BF16)
        mine_ref[:, at : at + step] = part[:rows]
        send_ref[:, at : at + step] = part[rows:]


def join_kernel(*refs):
    *in_refs, out_ref = refs
    out_ref[...] = jnp.concatenate([r[...] for r in in_refs], axis=0)


def add_kernel(a_ref, b_ref, *out_refs):
    total = (a_ref[...].astype(F32) + b_ref[...].astype(F32)).astype(BF16)
    size = total.shape[0] // len(out_refs)
    for i, out_ref in enumerate(out_refs):
        out_ref[...] = total[i * size : (i + 1) * size]


def merge_kernel(cap, here_ref, partner_ref, mirror_ref, opposite_ref, *out_refs):
    rows = jnp.concatenate([r[...] for r in (here_ref, partner_ref, mirror_ref, opposite_ref)], axis=0)
    shape = (len(out_refs) * 2 * cap, rows.shape[0])
    block = here_ref.shape[0]
    r, m = iota(shape, 0), iota(shape, 1)
    same = ((m % block) // cap == r // (2 * cap)) & (m % cap == r % cap)
    same = same & (m // (2 * block) == (r % (2 * cap)) // cap)
    merged = dot(ones_at(same), rows).astype(BF16)
    for d, out_ref in enumerate(out_refs):
        out_ref[...] = merged[d * 2 * cap : (d + 1) * 2 * cap]


def final_b_kernel(experts, cap, at_ref, cot_ref, route_ref, *refs):
    *in_refs, out_ref = refs
    tokens = cot_ref.shape[0]
    count = len(in_refs)
    rows = jnp.concatenate([r[...] for r in in_refs], axis=0)
    route = route_ref[...]
    slot = column(slots_of(route, experts))
    m = iota((tokens, rows.shape[0]), 1)
    pair = at_ref[1] // 2 ^ ((m % (2 * cap)) // cap)
    expert = (at_ref[0] + m // (2 * cap)) % count * 2 + pair
    total = dot(ones_at((expert == column(route)) & (m % cap == slot)), rows)
    out_ref[...] = (cot_ref[...].astype(F32) + total).astype(BF16)


def pack_f_kernel(experts, cap, x_ref, meta_ref, out_ref):
    tokens, width = x_ref.shape
    rows, half = out_ref.shape
    route = meta_ref[0:1, :].astype(jnp.int32)
    slot = slots_of(route, experts)
    m = iota((rows, tokens), 0)
    table = (m // (4 * cap) == route) & (m % cap == slot)
    low = (m % (2 * cap)) // cap == 0
    total = dot(ones_at(table & low), x_ref[:, :half])
    total += dot(ones_at(table & ~low), x_ref[:, half:])
    out_ref[...] = total.astype(BF16)


def joined(rows, cap):
    count = rows.shape[0]
    shape = (count // 2, count)
    r, m = iota(shape, 0), iota(shape, 1)
    same = (m // (2 * cap) == r // cap) & (m % cap == r % cap)
    low = (m % (2 * cap)) // cap == 0
    parts = [dot(ones_at(same & half), rows).astype(BF16) for half in (low, ~low)]
    return jnp.concatenate(parts, axis=1)


def parted(low, high, cap, rows):
    shape = (rows, rows // 2)
    m, r = iota(shape, 0), iota(shape, 1)
    same = (m // (2 * cap) == r // cap) & (m % cap == r % cap)
    first = (m % (2 * cap)) // cap == 0
    return (dot(ones_at(same & first), low) + dot(ones_at(same & ~first), high)).astype(BF16)


def expert_f_kernel(cap, own_ref, oth_ref, wgu_ref, wd_ref, mine_ref, send_ref):
    rows, half = own_ref.shape
    hid = wd_ref.shape[0]
    values = jnp.concatenate([joined(own_ref[...], cap), joined(oth_ref[...], cap)], axis=0)
    pre = dot(values, wgu_ref[...])
    gate = pre[:, :hid]
    hidden = (gate / (1.0 + jnp.exp(-gate)) * pre[:, hid:]).astype(BF16)
    mid = rows // 2
    step = 256 if half % 256 == 0 else half
    for at in range(0, half, step):
        low, high = (
            dot(hidden, wd_ref[:, base + at : base + at + step]).astype(BF16) for base in (0, half)
        )
        mine_ref[:, at : at + step] = parted(low[:mid], high[:mid], cap, rows)
        send_ref[:, at : at + step] = parted(low[mid:], high[mid:], cap, rows)


def final_f_kernel(experts, cap, x_ref, meta_ref, back_ref, out_ref):
    tokens = x_ref.shape[0]
    rows, half = back_ref.shape
    meta = meta_ref[...]
    route = meta[0:1, :].astype(jnp.int32)
    slot = column(slots_of(route, experts))
    gate = column(meta[1:2, :])
    m = iota((tokens, rows), 1)
    table = (m // (4 * cap) == column(route)) & (m % cap == slot)
    low = (m % (2 * cap)) // cap == 0
    back = back_ref[...]
    for base, part in ((0, low), (half, ~low)):
        total = gate * dot(ones_at(table & part), back)
        x = x_ref[:, base : base + half].astype(F32)
        out_ref[:, base : base + half] = (x + total).astype(BF16)


def call(kernel, name, shapes, operands, flops, earlier=()):
    out = [jax.ShapeDtypeStruct(s, BF16) for s in shapes]
    nbytes = sum(a.size * a.dtype.itemsize for a in (*operands, *out))
    count = len(operands)

    def body(*refs):
        kernel(*refs[:count], *refs[count + len(earlier) :])

    return pl.pallas_call(
        body,
        out_shape=out,
        in_specs=[SMEM if a.ndim == 1 else VMEM for a in operands] + [ANY] * len(earlier),
        out_specs=[VMEM] * len(out),
        compiler_params=PARAMS,
        name=name,
        cost_estimate=pl.CostEstimate(
            flops=flops + int(HIDES.get(name, 0)), bytes_accessed=nbytes, transcendentals=0
        ),
    )(*operands, *earlier)


def moved(block, axis, to):
    return lax.ppermute(block, axis, [(i, to(i)) for i in range(lax.axis_size(axis))])


def swap_core(block):
    return moved(block, "c", lambda i: 1 - i)


def shift(block, distance):
    count = lax.axis_size("pp")
    return moved(block, "pp", lambda i: (i + distance) % count)


def along_x(blocks, sign):
    count = len(blocks)
    rest = [moved(b, "x", lambda i, d=d: (i + sign * d) % count) for d, b in enumerate(blocks) if d]
    return [blocks[0]] + rest


def after(value, *earlier):
    return pl.pallas_call(
        lambda *refs: None,
        out_shape=jax.ShapeDtypeStruct(value.shape, value.dtype),
        in_specs=[ANY] * (1 + len(earlier)),
        out_specs=ANY,
        input_output_aliases={0: 0},
        name="after",
    )(value, *earlier)


def exchange(rows, cap):
    width = rows.shape[1]
    blocks = rows.reshape(-1, 2 * cap, width)
    blocks = lax.all_to_all(blocks, ("x", "zh"), split_axis=0, concat_axis=0, tiled=True)
    return blocks.reshape(-1, width)


def partner(block):
    return moved(block, "zh", lambda i: i ^ 1)


def mirror(block):
    return moved(block, "zh", lambda i: 3 - i)


def opposite(block):
    return moved(block, "zh", lambda i: i ^ 2)


def shards(fwd_in, fwd_route, fwd_gate, bwd_cot, bwd_route, bwd_gate, saved_pre, w_gate_up, w_down):
    devices = lax.axis_size(("x", "zh", "c"))
    experts = devices // SPLIT
    cap = saved_pre.shape[2] // devices
    cot = bwd_cot[0]
    tokens, width = cot.shape
    hid = w_down.shape[1]
    wgu, wd = w_gate_up[0], w_down[0]
    at = jnp.stack([lax.axis_index(a) for a in ("x", "zh", "c")]).astype(jnp.int32)
    many = devices * cap
    few = many // 2
    half = (many, width // 2)
    block = few // Z_GROUPS

    def kernel(body, *head):
        return lambda *refs: body(*head, *refs)

    route_b, gate_b = bwd_route.reshape(1, tokens), bwd_gate.reshape(1, tokens)
    meta = jnp.concatenate(
        [fwd_route.reshape(1, tokens).astype(F32), fwd_gate.reshape(1, tokens)], axis=0
    )
    x = shift(fwd_in[0], 1)
    meta = shift(meta, 1)

    chunks = call(
        kernel(pack_b_kernel, experts, cap),
        "pack_b",
        [(2 * cap, width)] * (block // cap),
        (at, cot, route_b, gate_b),
        4 * block * tokens * width,
    )
    chunks = along_x(chunks, 1)
    here, away = call(
        kernel(pairs_kernel, cap), "pairs", [(block, width)] * 2, chunks, 4 * block * block * width
    )
    from_partner = partner(here)
    from_mirror, from_opposite = mirror(away), opposite(away)
    blocks = (here, from_partner, from_mirror, from_opposite)

    (packed,) = call(
        kernel(pack_f_kernel, experts, cap),
        "pack_f",
        [half],
        (x, meta),
        2 * many * tokens * width,
        earlier=(here,),
    )
    own_f = exchange(packed, cap)
    (own_b,) = call(join_kernel, "join_b", [(few, width)], blocks, few * width, earlier=(packed,))

    mine_b, send_b = call(
        kernel(expert_b_kernel, cap),
        "expert_b",
        [(few, width)] * 2,
        (at, own_b, swap_core(own_b), saved_pre[0, 0], wgu, wd),
        6 * many * hid * width,
    )
    here, to_partner, to_mirror, to_opposite = call(
        add_kernel, "add_b", [(block, width)] * Z_GROUPS, (mine_b, swap_core(send_b)), few * width
    )
    from_partner = partner(to_partner)
    from_mirror, from_opposite = mirror(to_mirror), opposite(to_opposite)
    chunks = call(
        kernel(merge_kernel, cap),
        "merge_b",
        [(2 * cap, width)] * (block // cap),
        (here, from_partner, from_mirror, from_opposite),
        4 * block * few * width,
    )
    chunks = along_x(chunks, -1)
    (out_b,) = call(
        kernel(final_b_kernel, experts, cap),
        "final_b",
        [(tokens, width)],
        (at, cot, route_b, *chunks),
        4 * block * tokens * width,
    )
    out_b = shift(out_b, -1)

    def chain(_, rows):
        mine, send = call(
            kernel(expert_f_kernel, cap),
            "expert_f",
            [half] * 2,
            (rows, swap_core(rows), wgu, wd),
            6 * many * hid * width,
        )
        return (mine.astype(F32) + swap_core(send).astype(F32)).astype(BF16)

    rounds = jnp.minimum(jnp.sum((fwd_route < experts).astype(jnp.int32)), 1)
    summed_f = lax.fori_loop(0, rounds, chain, own_f)
    back_f = exchange(summed_f, cap)
    (out_f,) = call(
        kernel(final_f_kernel, experts, cap),
        "final_f",
        [(tokens, width)],
        (x, meta, back_f),
        2 * many * tokens * width,
    )
    return out_f[None], out_b[None]


def solution(mesh):
    sections, members = mesh.devices.shape
    fine = Mesh(
        mesh.devices.reshape(sections, members // (Z_GROUPS * CORES), Z_GROUPS, CORES),
        ("pp", "x", "zh", "c"),
    )
    ep = ("x", "zh", "c")
    rows = P("pp", ep, None)
    return jax.shard_map(
        shards,
        mesh=fine,
        in_specs=(rows,) * 6 + (P("pp", ep, None, None), P(ep, None, None), P(ep, None, None)),
        out_specs=(rows, rows),
        check_vma=False,
    )
```

```python
import jax
import jax.numpy as jnp
from jax import lax
from jax.experimental import pallas as pl
from jax.experimental.pallas import tpu as pltpu
from jax.sharding import Mesh
from jax.sharding import PartitionSpec as P

CORES = 2
Z_GROUPS = 4
SPLIT = 4
HIDES = {"pack_b": 1e11, "pack_f": 1e11, "merge_b": 1e11}
F32 = jnp.float32
BF16 = jnp.bfloat16
VMEM = pl.BlockSpec(memory_space=pltpu.VMEM)
ANY = pl.BlockSpec(memory_space=pl.ANY)
SMEM = pl.BlockSpec(memory_space=pltpu.SMEM)
PARAMS = pltpu.CompilerParams(vmem_limit_bytes=44 * 1024 * 1024)


def iota(shape, axis):
    return lax.broadcasted_iota(jnp.int32, shape, axis)


def dot(a, b, dims=((1,), (0,))):
    return lax.dot_general(a, b, (dims, ((), ())), preferred_element_type=F32)


def ones_at(where):
    return jnp.where(where, 1.0, 0.0).astype(BF16)


def slots_of(route, experts):
    tokens = route.shape[1]
    onehot = jnp.where(iota((experts, tokens), 0) == route, 1.0, 0.0)
    shape = (tokens, tokens)
    before = dot(onehot.astype(BF16), ones_at(iota(shape, 0) < iota(shape, 1)))
    return jnp.sum(before * onehot, axis=0, keepdims=True).astype(jnp.int32)


def column(row):
    tokens = row.shape[1]
    shape = (tokens, tokens)
    on = iota(shape, 0) == iota(shape, 1)
    return jnp.sum(jnp.where(on, row, jnp.zeros((), row.dtype)), axis=1, keepdims=True)


def joined(rows, cap):
    count = rows.shape[0]
    shape = (count // 2, count)
    r, m = iota(shape, 0), iota(shape, 1)
    same = (m // (2 * cap) == r // cap) & (m % cap == r % cap)
    low = (m % (2 * cap)) // cap == 0
    parts = [dot(ones_at(same & half), rows).astype(BF16) for half in (low, ~low)]
    return jnp.concatenate(parts, axis=1)


def parted(low, high, cap, rows):
    shape = (rows, rows // 2)
    m, r = iota(shape, 0), iota(shape, 1)
    same = (m // (2 * cap) == r // cap) & (m % cap == r % cap)
    first = (m % (2 * cap)) // cap == 0
    return (dot(ones_at(same & first), low) + dot(ones_at(same & ~first), high)).astype(BF16)


def source_of(at_ref, d, block, count):
    return (at_ref[0] + count - d) % count, at_ref[1] ^ block ^ (block // 2)


def slab(refs):
    return jnp.concatenate([r[...] for r in refs], axis=0)


def cut(rows, refs):
    size = rows.shape[0] // len(refs)
    for i, ref in enumerate(refs):
        ref[...] = rows[i * size : (i + 1) * size]


def pack_b_kernel(experts, cap, cot_ref, route_ref, gate_ref, out_ref):
    tokens, width = cot_ref.shape
    rows, half = out_ref.shape
    scaled = (column(gate_ref[...]) * cot_ref[...].astype(F32)).astype(BF16)
    route = route_ref[...]
    slot = slots_of(route, experts)
    m = iota((rows, tokens), 0)
    table = (m // (4 * cap) == route) & (m % cap == slot)
    low = (m % (2 * cap)) // cap == 0
    total = dot(ones_at(table & low), scaled[:, :half])
    total += dot(ones_at(table & ~low), scaled[:, half:])
    out_ref[...] = total.astype(BF16)


def expert_b_kernel(cap, c_ref, own_ref, oth_ref, saved_ref, wgu_ref, wd_ref, mine_ref, send_ref):
    rows, half = own_ref.shape
    hid, width = wd_ref.shape
    values = jnp.concatenate([joined(own_ref[...], cap), joined(oth_ref[...], cap)], axis=0)
    dh = dot(values, wd_ref[...], ((1,), (1,)))
    r, p = iota((rows, rows), 0), iota((rows, rows), 1)
    core = jnp.where(r < rows // 2, c_ref[0], 1 - c_ref[0])
    r = r % (rows // 2)
    pick = (p // (2 * cap) == r // cap) & (p % cap == r % cap) & ((p % (2 * cap)) // cap == core)
    saved = dot(ones_at(pick), saved_ref[...])
    act = saved[:, :hid]
    lin = saved[:, hid:]
    sig = 1.0 / (1.0 + jnp.exp(-act))
    d_act = (dh * lin * sig * (1.0 + act * (1.0 - sig))).astype(BF16)
    d_lin = (dh * act * sig).astype(BF16)
    grads = jnp.concatenate([d_act, d_lin], axis=1)
    step = 256 if half % 256 == 0 else half
    for at in range(0, half, step):
        low, high = (
            dot(grads, wgu_ref[base + at : base + at + step, :], ((1,), (1,))).astype(BF16)
            for base in (0, half)
        )
        mid = rows // 2
        mine_ref[:, at : at + step] = parted(low[:mid], high[:mid], cap, rows)
        send_ref[:, at : at + step] = parted(low[mid:], high[mid:], cap, rows)


def split_b_kernel(cap, at_ref, rows_ref, *out_refs):
    rows = joined(rows_ref[...], cap)
    count = rows.shape[0] // (Z_GROUPS * cap)
    shape = (rows.shape[0], rows.shape[0])
    r, m = iota(shape, 0), iota(shape, 1)
    x, z = source_of(at_ref, (r // cap) % count, r // (count * cap), count)
    pick = m == (x * Z_GROUPS + z) * cap + r % cap
    cut(dot(ones_at(pick), rows).astype(BF16), out_refs)


def merge_kernel(cap, here_ref, partner_ref, mirror_ref, opposite_ref, *out_refs):
    rows = jnp.concatenate([r[...] for r in (here_ref, partner_ref, mirror_ref, opposite_ref)], axis=0)
    shape = (len(out_refs) * 2 * cap, rows.shape[0])
    block = here_ref.shape[0]
    r, m = iota(shape, 0), iota(shape, 1)
    same = ((m % block) // cap == r // (2 * cap)) & (m % cap == r % cap)
    same = same & (m // (2 * block) == (r % (2 * cap)) // cap)
    merged = dot(ones_at(same), rows).astype(BF16)
    for d, out_ref in enumerate(out_refs):
        out_ref[...] = merged[d * 2 * cap : (d + 1) * 2 * cap]


def final_b_kernel(experts, cap, at_ref, cot_ref, route_ref, *refs):
    *in_refs, out_ref = refs
    tokens = cot_ref.shape[0]
    count = len(in_refs)
    rows = jnp.concatenate([r[...] for r in in_refs], axis=0)
    route = route_ref[...]
    slot = column(slots_of(route, experts))
    m = iota((tokens, rows.shape[0]), 1)
    pair = at_ref[1] // 2 ^ ((m % (2 * cap)) // cap)
    expert = (at_ref[0] + m // (2 * cap)) % count * 2 + pair
    total = dot(ones_at((expert == column(route)) & (m % cap == slot)), rows)
    out_ref[...] = (cot_ref[...].astype(F32) + total).astype(BF16)


def pack_f_kernel(experts, cap, at_ref, x_ref, meta_ref, *out_refs):
    tokens = x_ref.shape[0]
    route = meta_ref[0:1, :].astype(jnp.int32)
    slot = slots_of(route, experts)
    count = len(out_refs)
    m = iota((count * 2 * cap, tokens), 0)
    pair = at_ref[1] // 2 ^ ((m % (2 * cap)) // cap)
    expert = (at_ref[0] + m // (2 * cap)) % count * 2 + pair
    packed = dot(ones_at((expert == route) & (m % cap == slot)), x_ref[...]).astype(BF16)
    cut(packed, out_refs)


def pairs_kernel(cap, *refs):
    *in_refs, own_ref, oth_ref = refs
    rows = slab(in_refs)
    shape = (own_ref.shape[0], rows.shape[0])
    r, m = iota(shape, 0), iota(shape, 1)
    same = (m // (2 * cap) == r // cap) & (m % cap == r % cap)
    own = (m % (2 * cap)) // cap == 0
    own_ref[...] = dot(ones_at(same & own), rows).astype(BF16)
    oth_ref[...] = dot(ones_at(same & ~own), rows).astype(BF16)


def join_kernel(*refs):
    refs[-1][...] = slab(refs[:-1])


def expert_f_kernel(own_ref, oth_ref, wgu_ref, wd_ref, mine_ref, send_ref):
    rows = own_ref.shape[0]
    hid, width = wd_ref.shape
    pre = dot(slab((own_ref, oth_ref)), wgu_ref[...])
    gate = pre[:, :hid]
    hidden = (gate / (1.0 + jnp.exp(-gate)) * pre[:, hid:]).astype(BF16)
    step = 512 if width % 512 == 0 else width
    for at in range(0, width, step):
        part = dot(hidden, wd_ref[:, at : at + step]).astype(BF16)
        mine_ref[:, at : at + step] = part[:rows]
        send_ref[:, at : at + step] = part[rows:]


def add_kernel(a_ref, b_ref, *out_refs):
    cut((a_ref[...].astype(F32) + b_ref[...].astype(F32)).astype(BF16), out_refs)


def spread_f_kernel(cap, at_ref, *refs):
    *in_refs, out_ref = refs
    rows = slab(in_refs)
    many, half = out_ref.shape
    count = rows.shape[0] // (Z_GROUPS * cap)
    shape = (many, rows.shape[0])
    m, r = iota(shape, 0), iota(shape, 1)
    x, z = source_of(at_ref, (r // cap) % count, r // (count * cap), count)
    pick = (m // (2 * cap) == x * Z_GROUPS + z) & (m % cap == r % cap)
    low = (m % (2 * cap)) // cap == 0
    total = dot(ones_at(pick & low), rows[:, :half]) + dot(ones_at(pick & ~low), rows[:, half:])
    out_ref[...] = total.astype(BF16)


def final_f_kernel(experts, cap, x_ref, meta_ref, back_ref, out_ref):
    tokens = x_ref.shape[0]
    rows, half = back_ref.shape
    meta = meta_ref[...]
    route = meta[0:1, :].astype(jnp.int32)
    slot = column(slots_of(route, experts))
    gate = column(meta[1:2, :])
    m = iota((tokens, rows), 1)
    table = (m // (4 * cap) == column(route)) & (m % cap == slot)
    low = (m % (2 * cap)) // cap == 0
    back = back_ref[...]
    for base, part in ((0, low), (half, ~low)):
        total = gate * dot(ones_at(table & part), back)
        x = x_ref[:, base : base + half].astype(F32)
        out_ref[:, base : base + half] = (x + total).astype(BF16)


def call(kernel, name, shapes, operands, flops, earlier=()):
    out = [jax.ShapeDtypeStruct(s, BF16) for s in shapes]
    nbytes = sum(a.size * a.dtype.itemsize for a in (*operands, *out))
    count = len(operands)

    def body(*refs):
        kernel(*refs[:count], *refs[count + len(earlier) :])

    return pl.pallas_call(
        body,
        out_shape=out,
        in_specs=[SMEM if a.ndim == 1 else VMEM for a in operands] + [ANY] * len(earlier),
        out_specs=[VMEM] * len(out),
        compiler_params=PARAMS,
        name=name,
        cost_estimate=pl.CostEstimate(
            flops=flops + int(HIDES.get(name, 0)), bytes_accessed=nbytes, transcendentals=0
        ),
    )(*operands, *earlier)


def moved(block, axis, to):
    return lax.ppermute(block, axis, [(i, to(i)) for i in range(lax.axis_size(axis))])


def swap_core(block):
    return moved(block, "c", lambda i: 1 - i)


def shift(block, distance):
    count = lax.axis_size("pp")
    return moved(block, "pp", lambda i: (i + distance) % count)


def along_x(blocks, sign):
    count = len(blocks)
    rest = [moved(b, "x", lambda i, d=d: (i + sign * d) % count) for d, b in enumerate(blocks) if d]
    return [blocks[0]] + rest


def exchange(rows, cap):
    width = rows.shape[1]
    blocks = rows.reshape(-1, 2 * cap, width)
    blocks = lax.all_to_all(blocks, ("x", "zh"), split_axis=0, concat_axis=0, tiled=True)
    return blocks.reshape(-1, width)


def partner(block):
    return moved(block, "zh", lambda i: i ^ 1)


def mirror(block):
    return moved(block, "zh", lambda i: 3 - i)


def opposite(block):
    return moved(block, "zh", lambda i: i ^ 2)


def shards(fwd_in, fwd_route, fwd_gate, bwd_cot, bwd_route, bwd_gate, saved_pre, w_gate_up, w_down):
    devices = lax.axis_size(("x", "zh", "c"))
    experts = devices // SPLIT
    cap = saved_pre.shape[2] // devices
    cot = bwd_cot[0]
    tokens, width = cot.shape
    hid = w_down.shape[1]
    wgu, wd = w_gate_up[0], w_down[0]
    at = jnp.stack([lax.axis_index(a) for a in ("x", "zh", "c")]).astype(jnp.int32)
    many = devices * cap
    few = many // 2
    half = (many, width // 2)
    block = few // Z_GROUPS

    def kernel(body, *head):
        return lambda *refs: body(*head, *refs)

    route_b, gate_b = bwd_route.reshape(1, tokens), bwd_gate.reshape(1, tokens)
    meta = jnp.concatenate(
        [fwd_route.reshape(1, tokens).astype(F32), fwd_gate.reshape(1, tokens)], axis=0
    )
    x = shift(fwd_in[0], 1)
    meta = shift(meta, 1)
    core = at[2:]
    rounds = jnp.minimum(jnp.sum((bwd_route < experts).astype(jnp.int32)), 1)

    (packed,) = call(
        kernel(pack_b_kernel, experts, cap),
        "pack_b",
        [half],
        (cot, route_b, gate_b),
        2 * many * tokens * width,
    )
    own_b = exchange(packed, cap)

    chunks = call(
        kernel(pack_f_kernel, experts, cap),
        "pack_f",
        [(2 * cap, width)] * (block // cap),
        (at, x, meta),
        4 * block * tokens * width,
        earlier=(packed,),
    )
    chunks = along_x(chunks, 1)
    here, away = call(
        kernel(pairs_kernel, cap), "pairs_f", [(block, width)] * 2, chunks, 4 * block * block * width
    )
    blocks_f = (here, partner(here), mirror(away), opposite(away))

    def chain_b(_, rows):
        mine, send = call(
            kernel(expert_b_kernel, cap),
            "expert_b",
            [half] * 2,
            (core, rows, swap_core(rows), saved_pre[0, 0], wgu, wd),
            6 * many * hid * width,
        )
        return (mine.astype(F32) + swap_core(send).astype(F32)).astype(BF16)

    summed_b = lax.fori_loop(0, rounds, chain_b, own_b)
    here, to_partner, to_mirror, to_opposite = call(
        kernel(split_b_kernel, cap),
        "split_b",
        [(block, width)] * Z_GROUPS,
        (at, summed_b),
        2 * few * many * width,
    )
    blocks_b = (here, partner(to_partner), mirror(to_mirror), opposite(to_opposite))

    def chain_f(_, blocks):
        (own,) = call(join_kernel, "join_f", [(few, width)], blocks, few * width)
        mine, send = call(
            expert_f_kernel, "expert_f", [(few, width)] * 2, (own, swap_core(own), wgu, wd), 6 * many * hid * width
        )
        return tuple(
            call(add_kernel, "add_f", [(block, width)] * Z_GROUPS, (mine, swap_core(send)), few * width)
        )

    summed_f = lax.fori_loop(0, rounds, chain_f, blocks_f)
    (spread,) = call(
        kernel(spread_f_kernel, cap), "spread_f", [half], (at, *summed_f), 2 * few * many * width
    )
    back_f = exchange(spread, cap)

    chunks = call(
        kernel(merge_kernel, cap),
        "merge_b",
        [(2 * cap, width)] * (block // cap),
        blocks_b,
        4 * block * few * width,
    )
    chunks = along_x(chunks, -1)
    (out_b,) = call(
        kernel(final_b_kernel, experts, cap),
        "final_b",
        [(tokens, width)],
        (at, cot, route_b, *chunks),
        4 * block * tokens * width,
    )
    out_b = shift(out_b, -1)
    (out_f,) = call(
        kernel(final_f_kernel, experts, cap),
        "final_f",
        [(tokens, width)],
        (x, meta, back_f),
        2 * many * tokens * width,
    )
    return out_f[None], out_b[None]


def solution(mesh):
    sections, members = mesh.devices.shape
    fine = Mesh(
        mesh.devices.reshape(sections, members // (Z_GROUPS * CORES), Z_GROUPS, CORES),
        ("pp", "x", "zh", "c"),
    )
    ep = ("x", "zh", "c")
    rows = P("pp", ep, None)
    return jax.shard_map(
        shards,
        mesh=fine,
        in_specs=(rows,) * 6 + (P("pp", ep, None, None), P(ep, None, None), P(ep, None, None)),
        out_specs=(rows, rows),
        check_vma=False,
    )
```

```python
import jax
import jax.numpy as jnp
from jax import lax
from jax.experimental import pallas as pl
from jax.experimental.pallas import tpu as pltpu
from jax.sharding import Mesh
from jax.sharding import PartitionSpec as P

CORES = 2
Z_GROUPS = 4
SPLIT = 4
HIDES = {"pack_b": 1e11, "pack_f": 1e11, "merge_b": 1e11}
F32 = jnp.float32
BF16 = jnp.bfloat16
VMEM = pl.BlockSpec(memory_space=pltpu.VMEM)
ANY = pl.BlockSpec(memory_space=pl.ANY)
SMEM = pl.BlockSpec(memory_space=pltpu.SMEM)
PARAMS = pltpu.CompilerParams(vmem_limit_bytes=44 * 1024 * 1024)


def iota(shape, axis):
    return lax.broadcasted_iota(jnp.int32, shape, axis)


def dot(a, b, dims=((1,), (0,))):
    return lax.dot_general(a, b, (dims, ((), ())), preferred_element_type=F32)


def ones_at(where):
    return jnp.where(where, 1.0, 0.0).astype(BF16)


def slots_of(route, experts):
    tokens = route.shape[1]
    onehot = jnp.where(iota((experts, tokens), 0) == route, 1.0, 0.0)
    shape = (tokens, tokens)
    before = dot(onehot.astype(BF16), ones_at(iota(shape, 0) < iota(shape, 1)))
    return jnp.sum(before * onehot, axis=0, keepdims=True).astype(jnp.int32)


def column(row):
    tokens = row.shape[1]
    shape = (tokens, tokens)
    on = iota(shape, 0) == iota(shape, 1)
    return jnp.sum(jnp.where(on, row, jnp.zeros((), row.dtype)), axis=1, keepdims=True)


def joined(rows, cap):
    count = rows.shape[0]
    shape = (count // 2, count)
    r, m = iota(shape, 0), iota(shape, 1)
    same = (m // (2 * cap) == r // cap) & (m % cap == r % cap)
    low = (m % (2 * cap)) // cap == 0
    parts = [dot(ones_at(same & half), rows).astype(BF16) for half in (low, ~low)]
    return jnp.concatenate(parts, axis=1)


def parted(low, high, cap, rows):
    shape = (rows, rows // 2)
    m, r = iota(shape, 0), iota(shape, 1)
    same = (m // (2 * cap) == r // cap) & (m % cap == r % cap)
    first = (m % (2 * cap)) // cap == 0
    return (dot(ones_at(same & first), low) + dot(ones_at(same & ~first), high)).astype(BF16)


def source_of(at_ref, d, block, count):
    return (at_ref[0] + count - d) % count, at_ref[1] ^ block ^ (block // 2)


def stream(far_refs, near_refs, sems):
    copies = [
        pltpu.make_async_copy(far, near, sems.at[i])
        for i, (far, near) in enumerate(zip(far_refs, near_refs))
    ]
    for copy in copies:
        copy.start()
    return copies


def slab(refs):
    return jnp.concatenate([r[...] for r in refs], axis=0)


def cut(rows, refs):
    size = rows.shape[0] // len(refs)
    for i, ref in enumerate(refs):
        ref[...] = rows[i * size : (i + 1) * size]


def pack_b_kernel(experts, cap, cot_ref, route_ref, gate_ref, out_ref):
    tokens, width = cot_ref.shape
    rows, half = out_ref.shape
    scaled = (column(gate_ref[...]) * cot_ref[...].astype(F32)).astype(BF16)
    route = route_ref[...]
    slot = slots_of(route, experts)
    m = iota((rows, tokens), 0)
    table = (m // (4 * cap) == route) & (m % cap == slot)
    low = (m % (2 * cap)) // cap == 0
    total = dot(ones_at(table & low), scaled[:, :half])
    total += dot(ones_at(table & ~low), scaled[:, half:])
    out_ref[...] = total.astype(BF16)


def expert_b_kernel(cap, c_ref, own_ref, oth_ref, *refs):
    far, (mine_ref, send_ref), near, sems = refs[:3], refs[3:5], refs[5:8], refs[8]
    wd_ref, saved_ref, wgu_ref = near
    wd_copy, saved_copy, wgu_copy = stream(far, near, sems)
    rows, half = own_ref.shape
    hid, width = wd_ref.shape
    values = jnp.concatenate([joined(own_ref[...], cap), joined(oth_ref[...], cap)], axis=0)
    wd_copy.wait()
    dh = dot(values, wd_ref[...], ((1,), (1,)))
    r, p = iota((rows, rows), 0), iota((rows, rows), 1)
    core = jnp.where(r < rows // 2, c_ref[0], 1 - c_ref[0])
    r = r % (rows // 2)
    pick = (p // (2 * cap) == r // cap) & (p % cap == r % cap) & ((p % (2 * cap)) // cap == core)
    saved_copy.wait()
    saved = dot(ones_at(pick), saved_ref[...])
    act = saved[:, :hid]
    lin = saved[:, hid:]
    sig = 1.0 / (1.0 + jnp.exp(-act))
    d_act = (dh * lin * sig * (1.0 + act * (1.0 - sig))).astype(BF16)
    d_lin = (dh * act * sig).astype(BF16)
    grads = jnp.concatenate([d_act, d_lin], axis=1)
    wgu_copy.wait()
    step = 256 if half % 256 == 0 else half
    for at in range(0, half, step):
        low, high = (
            dot(grads, wgu_ref[base + at : base + at + step, :], ((1,), (1,))).astype(BF16)
            for base in (0, half)
        )
        mid = rows // 2
        mine_ref[:, at : at + step] = parted(low[:mid], high[:mid], cap, rows)
        send_ref[:, at : at + step] = parted(low[mid:], high[mid:], cap, rows)


def split_b_kernel(cap, at_ref, rows_ref, *out_refs):
    rows = joined(rows_ref[...], cap)
    count = rows.shape[0] // (Z_GROUPS * cap)
    shape = (rows.shape[0], rows.shape[0])
    r, m = iota(shape, 0), iota(shape, 1)
    x, z = source_of(at_ref, (r // cap) % count, r // (count * cap), count)
    pick = m == (x * Z_GROUPS + z) * cap + r % cap
    cut(dot(ones_at(pick), rows).astype(BF16), out_refs)


def merge_kernel(cap, here_ref, partner_ref, mirror_ref, opposite_ref, *out_refs):
    rows = jnp.concatenate([r[...] for r in (here_ref, partner_ref, mirror_ref, opposite_ref)], axis=0)
    shape = (len(out_refs) * 2 * cap, rows.shape[0])
    block = here_ref.shape[0]
    r, m = iota(shape, 0), iota(shape, 1)
    same = ((m % block) // cap == r // (2 * cap)) & (m % cap == r % cap)
    same = same & (m // (2 * block) == (r % (2 * cap)) // cap)
    merged = dot(ones_at(same), rows).astype(BF16)
    for d, out_ref in enumerate(out_refs):
        out_ref[...] = merged[d * 2 * cap : (d + 1) * 2 * cap]


def final_b_kernel(experts, cap, at_ref, cot_ref, route_ref, *refs):
    *in_refs, out_ref = refs
    tokens = cot_ref.shape[0]
    count = len(in_refs)
    rows = jnp.concatenate([r[...] for r in in_refs], axis=0)
    route = route_ref[...]
    slot = column(slots_of(route, experts))
    m = iota((tokens, rows.shape[0]), 1)
    pair = at_ref[1] // 2 ^ ((m % (2 * cap)) // cap)
    expert = (at_ref[0] + m // (2 * cap)) % count * 2 + pair
    total = dot(ones_at((expert == column(route)) & (m % cap == slot)), rows)
    out_ref[...] = (cot_ref[...].astype(F32) + total).astype(BF16)


def pack_f_kernel(experts, cap, at_ref, x_ref, route_ref, *out_refs):
    tokens = x_ref.shape[0]
    route = route_ref[...]
    slot = slots_of(route, experts)
    count = len(out_refs)
    m = iota((count * 2 * cap, tokens), 0)
    pair = at_ref[1] // 2 ^ ((m % (2 * cap)) // cap)
    expert = (at_ref[0] + m // (2 * cap)) % count * 2 + pair
    packed = dot(ones_at((expert == route) & (m % cap == slot)), x_ref[...]).astype(BF16)
    cut(packed, out_refs)


def pairs_kernel(cap, *refs):
    *in_refs, own_ref, oth_ref = refs
    rows = slab(in_refs)
    shape = (own_ref.shape[0], rows.shape[0])
    r, m = iota(shape, 0), iota(shape, 1)
    same = (m // (2 * cap) == r // cap) & (m % cap == r % cap)
    own = (m % (2 * cap)) // cap == 0
    own_ref[...] = dot(ones_at(same & own), rows).astype(BF16)
    oth_ref[...] = dot(ones_at(same & ~own), rows).astype(BF16)


def join_kernel(*refs):
    refs[-1][...] = slab(refs[:-1])


def expert_f_kernel(own_ref, oth_ref, *refs):
    far, (mine_ref, send_ref), near, sems = refs[:2], refs[2:4], refs[4:6], refs[6]
    wgu_ref, wd_ref = near
    wgu_copy, wd_copy = stream(far, near, sems)
    rows = own_ref.shape[0]
    hid, width = wd_ref.shape
    values = slab((own_ref, oth_ref))
    wgu_copy.wait()
    pre = dot(values, wgu_ref[...])
    gate = pre[:, :hid]
    hidden = (gate / (1.0 + jnp.exp(-gate)) * pre[:, hid:]).astype(BF16)
    wd_copy.wait()
    step = 512 if width % 512 == 0 else width
    for at in range(0, width, step):
        part = dot(hidden, wd_ref[:, at : at + step]).astype(BF16)
        mine_ref[:, at : at + step] = part[:rows]
        send_ref[:, at : at + step] = part[rows:]


def add_kernel(a_ref, b_ref, *out_refs):
    cut((a_ref[...].astype(F32) + b_ref[...].astype(F32)).astype(BF16), out_refs)


def spread_f_kernel(cap, at_ref, *refs):
    *in_refs, out_ref = refs
    rows = slab(in_refs)
    many, half = out_ref.shape
    count = rows.shape[0] // (Z_GROUPS * cap)
    shape = (many, rows.shape[0])
    m, r = iota(shape, 0), iota(shape, 1)
    x, z = source_of(at_ref, (r // cap) % count, r // (count * cap), count)
    pick = (m // (2 * cap) == x * Z_GROUPS + z) & (m % cap == r % cap)
    low = (m % (2 * cap)) // cap == 0
    total = dot(ones_at(pick & low), rows[:, :half]) + dot(ones_at(pick & ~low), rows[:, half:])
    out_ref[...] = total.astype(BF16)


def final_f_kernel(experts, cap, x_ref, route_ref, gate_ref, back_ref, out_ref):
    tokens = x_ref.shape[0]
    rows, half = back_ref.shape
    route = route_ref[...]
    slot = column(slots_of(route, experts))
    gate = column(gate_ref[...])
    m = iota((tokens, rows), 1)
    table = (m // (4 * cap) == column(route)) & (m % cap == slot)
    low = (m % (2 * cap)) // cap == 0
    back = back_ref[...]
    for base, part in ((0, low), (half, ~low)):
        total = gate * dot(ones_at(table & part), back)
        x = x_ref[:, base : base + half].astype(F32)
        out_ref[:, base : base + half] = (x + total).astype(BF16)


def call(kernel, name, shapes, operands, flops, earlier=(), streamed=0):
    out = [jax.ShapeDtypeStruct(s, BF16) for s in shapes]
    nbytes = sum(a.size * a.dtype.itemsize for a in (*operands, *out))
    count = len(operands)
    far = operands[count - streamed :]

    def body(*refs):
        kernel(*refs[:count], *refs[count + len(earlier) :])

    scratch = [pltpu.VMEM(a.shape, a.dtype) for a in far]
    return pl.pallas_call(
        body,
        out_shape=out,
        in_specs=[SMEM if a.ndim == 1 else VMEM for a in operands[: count - streamed]]
        + [ANY] * (streamed + len(earlier)),
        out_specs=[VMEM] * len(out),
        scratch_shapes=scratch + [pltpu.SemaphoreType.DMA((streamed,))] * (streamed > 0),
        compiler_params=PARAMS,
        name=name,
        cost_estimate=pl.CostEstimate(
            flops=flops + int(HIDES.get(name, 0)), bytes_accessed=nbytes, transcendentals=0
        ),
    )(*operands, *earlier)


def moved(block, axis, to):
    return lax.ppermute(block, axis, [(i, to(i)) for i in range(lax.axis_size(axis))])


def swap_core(block):
    return moved(block, "c", lambda i: 1 - i)


def shift(block, distance):
    count = lax.axis_size("pp")
    return moved(block, "pp", lambda i: (i + distance) % count)


def along_x(blocks, sign):
    count = len(blocks)
    rest = [moved(b, "x", lambda i, d=d: (i + sign * d) % count) for d, b in enumerate(blocks) if d]
    return [blocks[0]] + rest


def exchange(rows, cap):
    width = rows.shape[1]
    blocks = rows.reshape(-1, 2 * cap, width)
    blocks = lax.all_to_all(blocks, ("x", "zh"), split_axis=0, concat_axis=0, tiled=True)
    return blocks.reshape(-1, width)


def partner(block):
    return moved(block, "zh", lambda i: i ^ 1)


def mirror(block):
    return moved(block, "zh", lambda i: 3 - i)


def opposite(block):
    return moved(block, "zh", lambda i: i ^ 2)


def shards(fwd_in, fwd_route, fwd_gate, bwd_cot, bwd_route, bwd_gate, saved_pre, w_gate_up, w_down):
    devices = lax.axis_size(("x", "zh", "c"))
    experts = devices // SPLIT
    cap = saved_pre.shape[2] // devices
    cot = bwd_cot[0]
    tokens, width = cot.shape
    hid = w_down.shape[1]
    wgu, wd = w_gate_up[0], w_down[0]
    at = jnp.stack([lax.axis_index(a) for a in ("x", "zh", "c")]).astype(jnp.int32)
    many = devices * cap
    few = many // 2
    half = (many, width // 2)
    block = few // Z_GROUPS

    def kernel(body, *head):
        return lambda *refs: body(*head, *refs)

    route_b, gate_b = bwd_route.reshape(1, tokens), bwd_gate.reshape(1, tokens)
    x = shift(fwd_in[0], 1)
    route_f = shift(fwd_route.reshape(1, tokens), 1)
    gate_f = shift(fwd_gate.reshape(1, tokens), 1)
    core = at[2:]
    rounds = jnp.minimum(jnp.sum((bwd_route < experts).astype(jnp.int32)), 1)

    (packed,) = call(
        kernel(pack_b_kernel, experts, cap),
        "pack_b",
        [half],
        (cot, route_b, gate_b),
        2 * many * tokens * width,
    )
    own_b = exchange(packed, cap)

    chunks = call(
        kernel(pack_f_kernel, experts, cap),
        "pack_f",
        [(2 * cap, width)] * (block // cap),
        (at, x, route_f),
        4 * block * tokens * width,
        earlier=(packed,),
    )
    chunks = along_x(chunks, 1)
    here, away = call(
        kernel(pairs_kernel, cap), "pairs_f", [(block, width)] * 2, chunks, 4 * block * block * width
    )
    blocks_f = (here, partner(here), mirror(away), opposite(away))

    def chain_b(_, rows):
        mine, send = call(
            kernel(expert_b_kernel, cap),
            "expert_b",
            [half] * 2,
            (core, rows, swap_core(rows), wd, saved_pre[0, 0], wgu),
            6 * many * hid * width,
            streamed=3,
        )
        return (mine.astype(F32) + swap_core(send).astype(F32)).astype(BF16)

    summed_b = lax.fori_loop(0, rounds, chain_b, own_b)
    here, to_partner, to_mirror, to_opposite = call(
        kernel(split_b_kernel, cap),
        "split_b",
        [(block, width)] * Z_GROUPS,
        (at, summed_b),
        2 * few * many * width,
    )
    blocks_b = (here, partner(to_partner), mirror(to_mirror), opposite(to_opposite))

    def chain_f(_, blocks):
        (own,) = call(join_kernel, "join_f", [(few, width)], blocks, few * width)
        mine, send = call(
            expert_f_kernel, "expert_f", [(few, width)] * 2, (own, swap_core(own), wgu, wd), 6 * many * hid * width, streamed=2
        )
        return tuple(
            call(add_kernel, "add_f", [(block, width)] * Z_GROUPS, (mine, swap_core(send)), few * width)
        )

    summed_f = lax.fori_loop(0, rounds, chain_f, blocks_f)
    (spread,) = call(
        kernel(spread_f_kernel, cap), "spread_f", [half], (at, *summed_f), 2 * few * many * width
    )
    back_f = exchange(spread, cap)

    chunks = call(
        kernel(merge_kernel, cap),
        "merge_b",
        [(2 * cap, width)] * (block // cap),
        blocks_b,
        4 * block * few * width,
    )
    chunks = along_x(chunks, -1)
    (out_b,) = call(
        kernel(final_b_kernel, experts, cap),
        "final_b",
        [(tokens, width)],
        (at, cot, route_b, *chunks),
        4 * block * tokens * width,
    )
    out_b = shift(out_b, -1)
    (out_f,) = call(
        kernel(final_f_kernel, experts, cap),
        "final_f",
        [(tokens, width)],
        (x, route_f, gate_f, back_f),
        2 * many * tokens * width,
    )
    return out_f[None], out_b[None]


def solution(mesh):
    sections, members = mesh.devices.shape
    fine = Mesh(
        mesh.devices.reshape(sections, members // (Z_GROUPS * CORES), Z_GROUPS, CORES),
        ("pp", "x", "zh", "c"),
    )
    ep = ("x", "zh", "c")
    rows = P("pp", ep, None)
    return jax.shard_map(
        shards,
        mesh=fine,
        in_specs=(rows,) * 6 + (P("pp", ep, None, None), P(ep, None, None), P(ep, None, None)),
        out_specs=(rows, rows),
        check_vma=False,
    )
```

```python
import jax
import jax.numpy as jnp
from jax import lax
from jax.experimental import pallas as pl
from jax.experimental.pallas import tpu as pltpu
from jax.sharding import Mesh
from jax.sharding import PartitionSpec as P

CORES = 2
Z_GROUPS = 4
SPLIT = 4
HIDES = {"pack_b": 1e11, "pack_f": 1e11, "merge_b": 1e11}
F32 = jnp.float32
BF16 = jnp.bfloat16
VMEM = pl.BlockSpec(memory_space=pltpu.VMEM)
ANY = pl.BlockSpec(memory_space=pl.ANY)
SMEM = pl.BlockSpec(memory_space=pltpu.SMEM)
PARAMS = pltpu.CompilerParams(vmem_limit_bytes=44 * 1024 * 1024)


def iota(shape, axis):
    return lax.broadcasted_iota(jnp.int32, shape, axis)


def dot(a, b, dims=((1,), (0,))):
    return lax.dot_general(a, b, (dims, ((), ())), preferred_element_type=F32)


def ones_at(where):
    return jnp.where(where, 1.0, 0.0).astype(BF16)


def slots_of(route, experts):
    tokens = route.shape[1]
    onehot = jnp.where(iota((experts, tokens), 0) == route, 1.0, 0.0)
    shape = (tokens, tokens)
    before = dot(onehot.astype(BF16), ones_at(iota(shape, 0) < iota(shape, 1)))
    return jnp.sum(before * onehot, axis=0, keepdims=True).astype(jnp.int32)


def column(row):
    tokens = row.shape[1]
    shape = (tokens, tokens)
    on = iota(shape, 0) == iota(shape, 1)
    return jnp.sum(jnp.where(on, row, jnp.zeros((), row.dtype)), axis=1, keepdims=True)


def joined(rows, cap):
    count = rows.shape[0]
    shape = (count // 2, count)
    r, m = iota(shape, 0), iota(shape, 1)
    same = (m // (2 * cap) == r // cap) & (m % cap == r % cap)
    low = (m % (2 * cap)) // cap == 0
    parts = [dot(ones_at(same & half), rows).astype(BF16) for half in (low, ~low)]
    return jnp.concatenate(parts, axis=1)


def parted(low, high, cap, rows):
    shape = (rows, rows // 2)
    m, r = iota(shape, 0), iota(shape, 1)
    same = (m // (2 * cap) == r // cap) & (m % cap == r % cap)
    first = (m % (2 * cap)) // cap == 0
    return (dot(ones_at(same & first), low) + dot(ones_at(same & ~first), high)).astype(BF16)


def source_of(at_ref, d, block, count):
    return (at_ref[0] + count - d) % count, at_ref[1] ^ block ^ (block // 2)


def stream(far_refs, near_refs, sems):
    copies = [
        pltpu.make_async_copy(far, near, sems.at[i])
        for i, (far, near) in enumerate(zip(far_refs, near_refs))
    ]
    for copy in copies:
        copy.start()
    return copies


def slab(refs):
    return jnp.concatenate([r[...] for r in refs], axis=0)


def cut(rows, refs):
    size = rows.shape[0] // len(refs)
    for i, ref in enumerate(refs):
        ref[...] = rows[i * size : (i + 1) * size]


def pack_b_kernel(experts, cap, cot_ref, route_ref, gate_ref, out_ref):
    tokens, width = cot_ref.shape
    rows, half = out_ref.shape
    scaled = (column(gate_ref[...]) * cot_ref[...].astype(F32)).astype(BF16)
    route = route_ref[...]
    slot = slots_of(route, experts)
    m = iota((rows, tokens), 0)
    table = (m // (4 * cap) == route) & (m % cap == slot)
    low = (m % (2 * cap)) // cap == 0
    total = dot(ones_at(table & low), scaled[:, :half])
    total += dot(ones_at(table & ~low), scaled[:, half:])
    out_ref[...] = total.astype(BF16)


def expert_b_kernel(cap, c_ref, both_ref, *refs):
    far, (mine_ref, send_ref), near, sems = refs[:3], refs[3:5], refs[5:8], refs[8]
    wd_ref, saved_ref, wgu_ref = near
    wd_copy, saved_copy, wgu_copy = stream(far, near, sems)
    rows, half = mine_ref.shape
    hid, width = wd_ref.shape
    values = jnp.concatenate([joined(both_ref[:rows], cap), joined(both_ref[rows:], cap)], axis=0)
    wd_copy.wait()
    dh = dot(values, wd_ref[...], ((1,), (1,)))
    r, p = iota((rows, rows), 0), iota((rows, rows), 1)
    core = r // (rows // 2)
    r = r % (rows // 2)
    pick = (p // (2 * cap) == r // cap) & (p % cap == r % cap) & ((p % (2 * cap)) // cap == core)
    saved_copy.wait()
    saved = dot(ones_at(pick), saved_ref[...])
    act = saved[:, :hid]
    lin = saved[:, hid:]
    sig = 1.0 / (1.0 + jnp.exp(-act))
    d_act = (dh * lin * sig * (1.0 + act * (1.0 - sig))).astype(BF16)
    d_lin = (dh * act * sig).astype(BF16)
    grads = jnp.concatenate([d_act, d_lin], axis=1)
    wgu_copy.wait()
    step = 256 if half % 256 == 0 else half
    for at in range(0, half, step):
        low, high = (
            dot(grads, wgu_ref[base + at : base + at + step, :], ((1,), (1,))).astype(BF16)
            for base in (0, half)
        )
        mid = rows // 2
        first = parted(low[:mid], high[:mid], cap, rows)
        second = parted(low[mid:], high[mid:], cap, rows)
        mine_ref[:, at : at + step] = jnp.where(c_ref[0] == 0, first, second)
        send_ref[:, at : at + step] = jnp.where(c_ref[0] == 0, second, first)


def split_b_kernel(cap, at_ref, rows_ref, *out_refs):
    rows = joined(rows_ref[...], cap)
    count = rows.shape[0] // (Z_GROUPS * cap)
    shape = (rows.shape[0], rows.shape[0])
    r, m = iota(shape, 0), iota(shape, 1)
    x, z = source_of(at_ref, (r // cap) % count, r // (count * cap), count)
    pick = m == (x * Z_GROUPS + z) * cap + r % cap
    cut(dot(ones_at(pick), rows).astype(BF16), out_refs)


def merge_kernel(cap, here_ref, partner_ref, mirror_ref, opposite_ref, *out_refs):
    rows = jnp.concatenate([r[...] for r in (here_ref, partner_ref, mirror_ref, opposite_ref)], axis=0)
    shape = (len(out_refs) * 2 * cap, rows.shape[0])
    block = here_ref.shape[0]
    r, m = iota(shape, 0), iota(shape, 1)
    same = ((m % block) // cap == r // (2 * cap)) & (m % cap == r % cap)
    same = same & (m // (2 * block) == (r % (2 * cap)) // cap)
    merged = dot(ones_at(same), rows).astype(BF16)
    for d, out_ref in enumerate(out_refs):
        out_ref[...] = merged[d * 2 * cap : (d + 1) * 2 * cap]


def final_b_kernel(experts, cap, at_ref, cot_ref, route_ref, *refs):
    *in_refs, out_ref = refs
    tokens = cot_ref.shape[0]
    count = len(in_refs)
    rows = jnp.concatenate([r[...] for r in in_refs], axis=0)
    route = route_ref[...]
    slot = column(slots_of(route, experts))
    m = iota((tokens, rows.shape[0]), 1)
    pair = at_ref[1] // 2 ^ ((m % (2 * cap)) // cap)
    expert = (at_ref[0] + m // (2 * cap)) % count * 2 + pair
    total = dot(ones_at((expert == column(route)) & (m % cap == slot)), rows)
    out_ref[...] = (cot_ref[...].astype(F32) + total).astype(BF16)


def pack_f_kernel(experts, cap, at_ref, x_ref, route_ref, *out_refs):
    tokens = x_ref.shape[0]
    route = route_ref[...]
    slot = slots_of(route, experts)
    count = len(out_refs)
    m = iota((count * 2 * cap, tokens), 0)
    pair = at_ref[1] // 2 ^ ((m % (2 * cap)) // cap)
    expert = (at_ref[0] + m // (2 * cap)) % count * 2 + pair
    packed = dot(ones_at((expert == route) & (m % cap == slot)), x_ref[...]).astype(BF16)
    cut(packed, out_refs)


def pairs_kernel(cap, *refs):
    *in_refs, own_ref, oth_ref = refs
    rows = slab(in_refs)
    shape = (own_ref.shape[0], rows.shape[0])
    r, m = iota(shape, 0), iota(shape, 1)
    same = (m // (2 * cap) == r // cap) & (m % cap == r % cap)
    own = (m % (2 * cap)) // cap == 0
    own_ref[...] = dot(ones_at(same & own), rows).astype(BF16)
    oth_ref[...] = dot(ones_at(same & ~own), rows).astype(BF16)


def join_kernel(*refs):
    refs[-1][...] = slab(refs[:-1])


def expert_f_kernel(c_ref, both_ref, *refs):
    far, (mine_ref, send_ref), near, sems = refs[:2], refs[2:4], refs[4:6], refs[6]
    wgu_ref, wd_ref = near
    wgu_copy, wd_copy = stream(far, near, sems)
    rows = mine_ref.shape[0]
    hid, width = wd_ref.shape
    wgu_copy.wait()
    pre = dot(both_ref[...], wgu_ref[...])
    gate = pre[:, :hid]
    hidden = (gate / (1.0 + jnp.exp(-gate)) * pre[:, hid:]).astype(BF16)
    wd_copy.wait()
    step = 512 if width % 512 == 0 else width
    for at in range(0, width, step):
        part = dot(hidden, wd_ref[:, at : at + step]).astype(BF16)
        mine_ref[:, at : at + step] = jnp.where(c_ref[0] == 0, part[:rows], part[rows:])
        send_ref[:, at : at + step] = jnp.where(c_ref[0] == 0, part[rows:], part[:rows])


def add_kernel(a_ref, b_ref, *out_refs):
    cut((a_ref[...].astype(F32) + b_ref[...].astype(F32)).astype(BF16), out_refs)


def spread_f_kernel(cap, at_ref, *refs):
    *in_refs, out_ref = refs
    rows = slab(in_refs)
    many, half = out_ref.shape
    count = rows.shape[0] // (Z_GROUPS * cap)
    shape = (many, rows.shape[0])
    m, r = iota(shape, 0), iota(shape, 1)
    x, z = source_of(at_ref, (r // cap) % count, r // (count * cap), count)
    pick = (m // (2 * cap) == x * Z_GROUPS + z) & (m % cap == r % cap)
    low = (m % (2 * cap)) // cap == 0
    total = dot(ones_at(pick & low), rows[:, :half]) + dot(ones_at(pick & ~low), rows[:, half:])
    out_ref[...] = total.astype(BF16)


def final_f_kernel(experts, cap, x_ref, route_ref, gate_ref, back_ref, out_ref):
    tokens = x_ref.shape[0]
    rows, half = back_ref.shape
    route = route_ref[...]
    slot = column(slots_of(route, experts))
    gate = column(gate_ref[...])
    m = iota((tokens, rows), 1)
    table = (m // (4 * cap) == column(route)) & (m % cap == slot)
    low = (m % (2 * cap)) // cap == 0
    back = back_ref[...]
    for base, part in ((0, low), (half, ~low)):
        total = gate * dot(ones_at(table & part), back)
        x = x_ref[:, base : base + half].astype(F32)
        out_ref[:, base : base + half] = (x + total).astype(BF16)


def call(kernel, name, shapes, operands, flops, earlier=(), streamed=0):
    out = [jax.ShapeDtypeStruct(s, BF16) for s in shapes]
    nbytes = sum(a.size * a.dtype.itemsize for a in (*operands, *out))
    count = len(operands)
    far = operands[count - streamed :]

    def body(*refs):
        kernel(*refs[:count], *refs[count + len(earlier) :])

    scratch = [pltpu.VMEM(a.shape, a.dtype) for a in far]
    return pl.pallas_call(
        body,
        out_shape=out,
        in_specs=[SMEM if a.ndim == 1 else VMEM for a in operands[: count - streamed]]
        + [ANY] * (streamed + len(earlier)),
        out_specs=[VMEM] * len(out),
        scratch_shapes=scratch + [pltpu.SemaphoreType.DMA((streamed,))] * (streamed > 0),
        compiler_params=PARAMS,
        name=name,
        cost_estimate=pl.CostEstimate(
            flops=flops + int(HIDES.get(name, 0)), bytes_accessed=nbytes, transcendentals=0
        ),
    )(*operands, *earlier)


def moved(block, axis, to):
    return lax.ppermute(block, axis, [(i, to(i)) for i in range(lax.axis_size(axis))])


def both_cores(block):
    return lax.all_gather(block, "c", axis=0, tiled=True)


def swap_core(block):
    return moved(block, "c", lambda i: 1 - i)


def shift(block, distance):
    count = lax.axis_size("pp")
    return moved(block, "pp", lambda i: (i + distance) % count)


def along_x(blocks, sign):
    count = len(blocks)
    rest = [moved(b, "x", lambda i, d=d: (i + sign * d) % count) for d, b in enumerate(blocks) if d]
    return [blocks[0]] + rest


def exchange(rows, cap):
    width = rows.shape[1]
    blocks = rows.reshape(-1, 2 * cap, width)
    blocks = lax.all_to_all(blocks, ("x", "zh"), split_axis=0, concat_axis=0, tiled=True)
    return blocks.reshape(-1, width)


def partner(block):
    return moved(block, "zh", lambda i: i ^ 1)


def mirror(block):
    return moved(block, "zh", lambda i: 3 - i)


def opposite(block):
    return moved(block, "zh", lambda i: i ^ 2)


def shards(fwd_in, fwd_route, fwd_gate, bwd_cot, bwd_route, bwd_gate, saved_pre, w_gate_up, w_down):
    devices = lax.axis_size(("x", "zh", "c"))
    experts = devices // SPLIT
    cap = saved_pre.shape[2] // devices
    cot = bwd_cot[0]
    tokens, width = cot.shape
    hid = w_down.shape[1]
    wgu, wd = w_gate_up[0], w_down[0]
    at = jnp.stack([lax.axis_index(a) for a in ("x", "zh", "c")]).astype(jnp.int32)
    many = devices * cap
    few = many // 2
    half = (many, width // 2)
    block = few // Z_GROUPS

    def kernel(body, *head):
        return lambda *refs: body(*head, *refs)

    route_b, gate_b = bwd_route.reshape(1, tokens), bwd_gate.reshape(1, tokens)
    x = shift(fwd_in[0], 1)
    route_f = shift(fwd_route.reshape(1, tokens), 1)
    gate_f = shift(fwd_gate.reshape(1, tokens), 1)
    core = at[2:]
    rounds = jnp.minimum(jnp.sum((bwd_route < experts).astype(jnp.int32)), 1)

    (packed,) = call(
        kernel(pack_b_kernel, experts, cap),
        "pack_b",
        [half],
        (cot, route_b, gate_b),
        2 * many * tokens * width,
        earlier=(route_f,),
    )
    own_b = exchange(packed, cap)

    chunks = call(
        kernel(pack_f_kernel, experts, cap),
        "pack_f",
        [(2 * cap, width)] * (block // cap),
        (at, x, route_f),
        4 * block * tokens * width,
        earlier=(packed,),
    )
    chunks = along_x(chunks, 1)
    here, away = call(
        kernel(pairs_kernel, cap), "pairs_f", [(block, width)] * 2, chunks, 4 * block * block * width
    )
    blocks_f = (here, partner(here), mirror(away), opposite(away))

    def chain_b(_, rows):
        mine, send = call(
            kernel(expert_b_kernel, cap),
            "expert_b",
            [half] * 2,
            (core, both_cores(rows), wd, saved_pre[0, 0], wgu),
            6 * many * hid * width,
            streamed=3,
        )
        return (mine.astype(F32) + swap_core(send).astype(F32)).astype(BF16)

    summed_b = lax.fori_loop(0, rounds, chain_b, own_b)
    here, to_partner, to_mirror, to_opposite = call(
        kernel(split_b_kernel, cap),
        "split_b",
        [(block, width)] * Z_GROUPS,
        (at, summed_b),
        2 * few * many * width,
    )
    blocks_b = (here, partner(to_partner), mirror(to_mirror), opposite(to_opposite))

    def chain_f(_, blocks):
        (own,) = call(join_kernel, "join_f", [(few, width)], blocks, few * width)
        mine, send = call(
            expert_f_kernel, "expert_f", [(few, width)] * 2, (core, both_cores(own), wgu, wd), 6 * many * hid * width, streamed=2
        )
        return tuple(
            call(add_kernel, "add_f", [(block, width)] * Z_GROUPS, (mine, swap_core(send)), few * width)
        )

    summed_f = lax.fori_loop(0, rounds, chain_f, blocks_f)
    (spread,) = call(
        kernel(spread_f_kernel, cap), "spread_f", [half], (at, *summed_f), 2 * few * many * width
    )
    back_f = exchange(spread, cap)

    chunks = call(
        kernel(merge_kernel, cap),
        "merge_b",
        [(2 * cap, width)] * (block // cap),
        blocks_b,
        4 * block * few * width,
    )
    chunks = along_x(chunks, -1)
    (out_b,) = call(
        kernel(final_b_kernel, experts, cap),
        "final_b",
        [(tokens, width)],
        (at, cot, route_b, *chunks),
        4 * block * tokens * width,
    )
    out_b = shift(out_b, -1)
    (out_f,) = call(
        kernel(final_f_kernel, experts, cap),
        "final_f",
        [(tokens, width)],
        (x, route_f, gate_f, back_f),
        2 * many * tokens * width,
    )
    return out_f[None], out_b[None]


def solution(mesh):
    sections, members = mesh.devices.shape
    fine = Mesh(
        mesh.devices.reshape(sections, members // (Z_GROUPS * CORES), Z_GROUPS, CORES),
        ("pp", "x", "zh", "c"),
    )
    ep = ("x", "zh", "c")
    rows = P("pp", ep, None)
    return jax.shard_map(
        shards,
        mesh=fine,
        in_specs=(rows,) * 6 + (P("pp", ep, None, None), P(ep, None, None), P(ep, None, None)),
        out_specs=(rows, rows),
        check_vma=False,
    )
```

```python
import jax
import jax.numpy as jnp
from jax import lax
from jax.experimental import pallas as pl
from jax.experimental.pallas import tpu as pltpu
from jax.sharding import Mesh
from jax.sharding import PartitionSpec as P

CORES = 2
Z_GROUPS = 4
SPLIT = 4
HIDES = {"pack_b": 1e11, "pack_f": 1e11, "merge_b": 1e11}
F32 = jnp.float32
BF16 = jnp.bfloat16
VMEM = pl.BlockSpec(memory_space=pltpu.VMEM)
ANY = pl.BlockSpec(memory_space=pl.ANY)
SMEM = pl.BlockSpec(memory_space=pltpu.SMEM)
PARAMS = pltpu.CompilerParams(vmem_limit_bytes=44 * 1024 * 1024)


def iota(shape, axis):
    return lax.broadcasted_iota(jnp.int32, shape, axis)


def dot(a, b, dims=((1,), (0,))):
    return lax.dot_general(a, b, (dims, ((), ())), preferred_element_type=F32)


def ones_at(where):
    return jnp.where(where, 1.0, 0.0).astype(BF16)


def slots_of(route, experts):
    tokens = route.shape[1]
    onehot = jnp.where(iota((experts, tokens), 0) == route, 1.0, 0.0)
    shape = (tokens, tokens)
    before = dot(onehot.astype(BF16), ones_at(iota(shape, 0) < iota(shape, 1)))
    return jnp.sum(before * onehot, axis=0, keepdims=True).astype(jnp.int32)


def column(row):
    tokens = row.shape[1]
    shape = (tokens, tokens)
    on = iota(shape, 0) == iota(shape, 1)
    return jnp.sum(jnp.where(on, row, jnp.zeros((), row.dtype)), axis=1, keepdims=True)


def joined(rows, cap):
    count = rows.shape[0]
    shape = (count // 2, count)
    r, m = iota(shape, 0), iota(shape, 1)
    same = (m // (2 * cap) == r // cap) & (m % cap == r % cap)
    low = (m % (2 * cap)) // cap == 0
    parts = [dot(ones_at(same & half), rows).astype(BF16) for half in (low, ~low)]
    return jnp.concatenate(parts, axis=1)


def parted(low, high, cap, rows):
    shape = (rows, rows // 2)
    m, r = iota(shape, 0), iota(shape, 1)
    same = (m // (2 * cap) == r // cap) & (m % cap == r % cap)
    first = (m % (2 * cap)) // cap == 0
    return (dot(ones_at(same & first), low) + dot(ones_at(same & ~first), high)).astype(BF16)


def source_of(at_ref, d, block, count):
    return (at_ref[0] + count - d) % count, at_ref[1] ^ block ^ (block // 2)


def stream(far_refs, near_refs, sems):
    copies = [
        pltpu.make_async_copy(far, near, sems.at[i])
        for i, (far, near) in enumerate(zip(far_refs, near_refs))
    ]
    for copy in copies:
        copy.start()
    return copies


def slab(refs):
    return jnp.concatenate([r[...] for r in refs], axis=0)


def cut(rows, refs):
    size = rows.shape[0] // len(refs)
    for i, ref in enumerate(refs):
        ref[...] = rows[i * size : (i + 1) * size]


def pack_b_kernel(experts, cap, cot_ref, route_ref, gate_ref, out_ref):
    tokens, width = cot_ref.shape
    rows, half = out_ref.shape
    scaled = (column(gate_ref[...]) * cot_ref[...].astype(F32)).astype(BF16)
    route = route_ref[...]
    slot = slots_of(route, experts)
    m = iota((rows, tokens), 0)
    table = (m // (4 * cap) == route) & (m % cap == slot)
    low = (m % (2 * cap)) // cap == 0
    total = dot(ones_at(table & low), scaled[:, :half])
    total += dot(ones_at(table & ~low), scaled[:, half:])
    out_ref[...] = total.astype(BF16)


def expert_b_kernel(cap, c_ref, both_ref, *refs):
    far, (mine_ref, send_ref), near, sems = refs[:3], refs[3:5], refs[5:8], refs[8]
    wd_ref, saved_ref, wgu_ref = near
    wd_copy, saved_copy, wgu_copy = stream(far, near, sems)
    rows, half = mine_ref.shape
    hid, width = wd_ref.shape
    values = jnp.concatenate([joined(both_ref[:rows], cap), joined(both_ref[rows:], cap)], axis=0)
    wd_copy.wait()
    dh = dot(values, wd_ref[...], ((1,), (1,)))
    r, p = iota((rows, rows), 0), iota((rows, rows), 1)
    core = r // (rows // 2)
    r = r % (rows // 2)
    pick = (p // (2 * cap) == r // cap) & (p % cap == r % cap) & ((p % (2 * cap)) // cap == core)
    saved_copy.wait()
    saved = dot(ones_at(pick), saved_ref[...])
    act = saved[:, :hid]
    lin = saved[:, hid:]
    sig = 1.0 / (1.0 + jnp.exp(-act))
    d_act = (dh * lin * sig * (1.0 + act * (1.0 - sig))).astype(BF16)
    d_lin = (dh * act * sig).astype(BF16)
    grads = jnp.concatenate([d_act, d_lin], axis=1)
    wgu_copy.wait()
    step = 256 if half % 256 == 0 else half
    for at in range(0, half, step):
        low, high = (
            dot(grads, wgu_ref[base + at : base + at + step, :], ((1,), (1,))).astype(BF16)
            for base in (0, half)
        )
        mid = rows // 2
        first = parted(low[:mid], high[:mid], cap, rows)
        second = parted(low[mid:], high[mid:], cap, rows)
        mine_ref[:, at : at + step] = jnp.where(c_ref[0] == 0, first, second)
        send_ref[:, at : at + step] = jnp.where(c_ref[0] == 0, second, first)


def split_b_kernel(cap, at_ref, rows_ref, *out_refs):
    rows = joined(rows_ref[...], cap)
    count = rows.shape[0] // (Z_GROUPS * cap)
    shape = (rows.shape[0], rows.shape[0])
    r, m = iota(shape, 0), iota(shape, 1)
    x, z = source_of(at_ref, (r // cap) % count, r // (count * cap), count)
    pick = m == (x * Z_GROUPS + z) * cap + r % cap
    cut(dot(ones_at(pick), rows).astype(BF16), out_refs)


def merge_kernel(cap, here_ref, partner_ref, mirror_ref, opposite_ref, *out_refs):
    rows = jnp.concatenate([r[...] for r in (here_ref, partner_ref, mirror_ref, opposite_ref)], axis=0)
    shape = (len(out_refs) * 2 * cap, rows.shape[0])
    block = here_ref.shape[0]
    r, m = iota(shape, 0), iota(shape, 1)
    same = ((m % block) // cap == r // (2 * cap)) & (m % cap == r % cap)
    same = same & (m // (2 * block) == (r % (2 * cap)) // cap)
    merged = dot(ones_at(same), rows).astype(BF16)
    for d, out_ref in enumerate(out_refs):
        out_ref[...] = merged[d * 2 * cap : (d + 1) * 2 * cap]


def final_b_kernel(experts, cap, at_ref, cot_ref, route_ref, *refs):
    *in_refs, out_ref = refs
    tokens = cot_ref.shape[0]
    count = len(in_refs)
    rows = jnp.concatenate([r[...] for r in in_refs], axis=0)
    route = route_ref[...]
    slot = column(slots_of(route, experts))
    m = iota((tokens, rows.shape[0]), 1)
    pair = at_ref[1] // 2 ^ ((m % (2 * cap)) // cap)
    expert = (at_ref[0] + m // (2 * cap)) % count * 2 + pair
    total = dot(ones_at((expert == column(route)) & (m % cap == slot)), rows)
    out_ref[...] = (cot_ref[...].astype(F32) + total).astype(BF16)


def pack_f_kernel(experts, cap, at_ref, x_ref, meta_ref, *out_refs):
    tokens = x_ref.shape[0]
    route = meta_ref[0:1, :].astype(jnp.int32)
    slot = slots_of(route, experts)
    count = len(out_refs)
    m = iota((count * 2 * cap, tokens), 0)
    pair = at_ref[1] // 2 ^ ((m % (2 * cap)) // cap)
    expert = (at_ref[0] + m // (2 * cap)) % count * 2 + pair
    packed = dot(ones_at((expert == route) & (m % cap == slot)), x_ref[...]).astype(BF16)
    cut(packed, out_refs)


def pairs_kernel(cap, *refs):
    *in_refs, own_ref, oth_ref = refs
    rows = slab(in_refs)
    shape = (own_ref.shape[0], rows.shape[0])
    r, m = iota(shape, 0), iota(shape, 1)
    same = (m // (2 * cap) == r // cap) & (m % cap == r % cap)
    own = (m % (2 * cap)) // cap == 0
    own_ref[...] = dot(ones_at(same & own), rows).astype(BF16)
    oth_ref[...] = dot(ones_at(same & ~own), rows).astype(BF16)


def join_kernel(*refs):
    refs[-1][...] = slab(refs[:-1])


def expert_f_kernel(c_ref, both_ref, *refs):
    far, (mine_ref, send_ref), near, sems = refs[:2], refs[2:4], refs[4:6], refs[6]
    wgu_ref, wd_ref = near
    wgu_copy, wd_copy = stream(far, near, sems)
    rows = mine_ref.shape[0]
    hid, width = wd_ref.shape
    wgu_copy.wait()
    pre = dot(both_ref[...], wgu_ref[...])
    gate = pre[:, :hid]
    hidden = (gate / (1.0 + jnp.exp(-gate)) * pre[:, hid:]).astype(BF16)
    wd_copy.wait()
    step = 512 if width % 512 == 0 else width
    for at in range(0, width, step):
        part = dot(hidden, wd_ref[:, at : at + step]).astype(BF16)
        mine_ref[:, at : at + step] = jnp.where(c_ref[0] == 0, part[:rows], part[rows:])
        send_ref[:, at : at + step] = jnp.where(c_ref[0] == 0, part[rows:], part[:rows])


def add_kernel(a_ref, b_ref, *out_refs):
    cut((a_ref[...].astype(F32) + b_ref[...].astype(F32)).astype(BF16), out_refs)


def spread_f_kernel(cap, at_ref, *refs):
    *in_refs, out_ref = refs
    rows = slab(in_refs)
    many, half = out_ref.shape
    count = rows.shape[0] // (Z_GROUPS * cap)
    shape = (many, rows.shape[0])
    m, r = iota(shape, 0), iota(shape, 1)
    x, z = source_of(at_ref, (r // cap) % count, r // (count * cap), count)
    pick = (m // (2 * cap) == x * Z_GROUPS + z) & (m % cap == r % cap)
    low = (m % (2 * cap)) // cap == 0
    total = dot(ones_at(pick & low), rows[:, :half]) + dot(ones_at(pick & ~low), rows[:, half:])
    out_ref[...] = total.astype(BF16)


def final_f_kernel(experts, cap, x_ref, meta_ref, back_ref, out_ref):
    tokens = x_ref.shape[0]
    rows, half = back_ref.shape
    meta = meta_ref[...]
    route = meta[0:1, :].astype(jnp.int32)
    slot = column(slots_of(route, experts))
    gate = column(meta[1:2, :])
    m = iota((tokens, rows), 1)
    table = (m // (4 * cap) == column(route)) & (m % cap == slot)
    low = (m % (2 * cap)) // cap == 0
    back = back_ref[...]
    for base, part in ((0, low), (half, ~low)):
        total = gate * dot(ones_at(table & part), back)
        x = x_ref[:, base : base + half].astype(F32)
        out_ref[:, base : base + half] = (x + total).astype(BF16)


def call(kernel, name, shapes, operands, flops, earlier=(), streamed=0):
    out = [jax.ShapeDtypeStruct(s, BF16) for s in shapes]
    nbytes = sum(a.size * a.dtype.itemsize for a in (*operands, *out))
    count = len(operands)
    far = operands[count - streamed :]

    def body(*refs):
        kernel(*refs[:count], *refs[count + len(earlier) :])

    scratch = [pltpu.VMEM(a.shape, a.dtype) for a in far]
    return pl.pallas_call(
        body,
        out_shape=out,
        in_specs=[SMEM if a.ndim == 1 else VMEM for a in operands[: count - streamed]]
        + [ANY] * (streamed + len(earlier)),
        out_specs=[VMEM] * len(out),
        scratch_shapes=scratch + [pltpu.SemaphoreType.DMA((streamed,))] * (streamed > 0),
        compiler_params=PARAMS,
        name=name,
        cost_estimate=pl.CostEstimate(
            flops=flops + int(HIDES.get(name, 0)), bytes_accessed=nbytes, transcendentals=0
        ),
    )(*operands, *earlier)


def moved(block, axis, to):
    return lax.ppermute(block, axis, [(i, to(i)) for i in range(lax.axis_size(axis))])


def both_cores(block):
    return lax.all_gather(block, "c", axis=0, tiled=True)


def swap_core(block):
    return moved(block, "c", lambda i: 1 - i)


def shift(block, distance):
    count = lax.axis_size("pp")
    return moved(block, "pp", lambda i: (i + distance) % count)


def along_x(blocks, sign):
    count = len(blocks)
    rest = [moved(b, "x", lambda i, d=d: (i + sign * d) % count) for d, b in enumerate(blocks) if d]
    return [blocks[0]] + rest


def exchange(rows, cap):
    width = rows.shape[1]
    blocks = rows.reshape(-1, 2 * cap, width)
    blocks = lax.all_to_all(blocks, ("x", "zh"), split_axis=0, concat_axis=0, tiled=True)
    return blocks.reshape(-1, width)


def partner(block):
    return moved(block, "zh", lambda i: i ^ 1)


def mirror(block):
    return moved(block, "zh", lambda i: 3 - i)


def opposite(block):
    return moved(block, "zh", lambda i: i ^ 2)


def shards(fwd_in, fwd_route, fwd_gate, bwd_cot, bwd_route, bwd_gate, saved_pre, w_gate_up, w_down):
    devices = lax.axis_size(("x", "zh", "c"))
    experts = devices // SPLIT
    cap = saved_pre.shape[2] // devices
    cot = bwd_cot[0]
    tokens, width = cot.shape
    hid = w_down.shape[1]
    wgu, wd = w_gate_up[0], w_down[0]
    at = jnp.stack([lax.axis_index(a) for a in ("x", "zh", "c")]).astype(jnp.int32)
    many = devices * cap
    few = many // 2
    half = (many, width // 2)
    block = few // Z_GROUPS

    def kernel(body, *head):
        return lambda *refs: body(*head, *refs)

    route_b, gate_b = bwd_route.reshape(1, tokens), bwd_gate.reshape(1, tokens)
    x = shift(fwd_in[0], 1)
    meta = jnp.concatenate(
        [fwd_route.reshape(1, tokens).astype(F32), fwd_gate.reshape(1, tokens)], axis=0
    )
    meta = shift(meta, 1)
    core = at[2:]
    rounds = jnp.minimum(jnp.sum((bwd_route < experts).astype(jnp.int32)), 1)

    (packed,) = call(
        kernel(pack_b_kernel, experts, cap),
        "pack_b",
        [half],
        (cot, route_b, gate_b),
        2 * many * tokens * width,
    )
    own_b = exchange(packed, cap)

    chunks = call(
        kernel(pack_f_kernel, experts, cap),
        "pack_f",
        [(2 * cap, width)] * (block // cap),
        (at, x, meta),
        4 * block * tokens * width,
        earlier=(packed,),
    )
    chunks = along_x(chunks, 1)
    here, away = call(
        kernel(pairs_kernel, cap), "pairs_f", [(block, width)] * 2, chunks, 4 * block * block * width
    )
    from_mirror = mirror(away)
    blocks_f = (here, partner(here), from_mirror, partner(from_mirror))

    def chain_b(_, rows):
        mine, send = call(
            kernel(expert_b_kernel, cap),
            "expert_b",
            [half] * 2,
            (core, both_cores(rows), wd, saved_pre[0, 0], wgu),
            6 * many * hid * width,
            streamed=3,
        )
        return (mine.astype(F32) + swap_core(send).astype(F32)).astype(BF16)

    summed_b = lax.fori_loop(0, rounds, chain_b, own_b)
    here, to_partner, to_mirror, to_opposite = call(
        kernel(split_b_kernel, cap),
        "split_b",
        [(block, width)] * Z_GROUPS,
        (at, summed_b),
        2 * few * many * width,
    )
    blocks_b = (here, partner(to_partner), mirror(to_mirror), opposite(to_opposite))

    def chain_f(_, blocks):
        (own,) = call(join_kernel, "join_f", [(few, width)], blocks, few * width)
        mine, send = call(
            expert_f_kernel, "expert_f", [(few, width)] * 2, (core, both_cores(own), wgu, wd), 6 * many * hid * width, streamed=2
        )
        return tuple(
            call(add_kernel, "add_f", [(block, width)] * Z_GROUPS, (mine, swap_core(send)), few * width)
        )

    summed_f = lax.fori_loop(0, rounds, chain_f, blocks_f)
    (spread,) = call(
        kernel(spread_f_kernel, cap), "spread_f", [half], (at, *summed_f), 2 * few * many * width
    )
    back_f = exchange(spread, cap)

    chunks = call(
        kernel(merge_kernel, cap),
        "merge_b",
        [(2 * cap, width)] * (block // cap),
        blocks_b,
        4 * block * few * width,
    )
    chunks = along_x(chunks, -1)
    (out_b,) = call(
        kernel(final_b_kernel, experts, cap),
        "final_b",
        [(tokens, width)],
        (at, cot, route_b, *chunks),
        4 * block * tokens * width,
    )
    out_b = shift(out_b, -1)
    (out_f,) = call(
        kernel(final_f_kernel, experts, cap),
        "final_f",
        [(tokens, width)],
        (x, meta, back_f),
        2 * many * tokens * width,
    )
    return out_f[None], out_b[None]


def solution(mesh):
    sections, members = mesh.devices.shape
    fine = Mesh(
        mesh.devices.reshape(sections, members // (Z_GROUPS * CORES), Z_GROUPS, CORES),
        ("pp", "x", "zh", "c"),
    )
    ep = ("x", "zh", "c")
    rows = P("pp", ep, None)
    return jax.shard_map(
        shards,
        mesh=fine,
        in_specs=(rows,) * 6 + (P("pp", ep, None, None), P(ep, None, None), P(ep, None, None)),
        out_specs=(rows, rows),
        check_vma=False,
    )
```

```python
import jax
import jax.numpy as jnp
from jax import lax
from jax.experimental import pallas as pl
from jax.experimental.pallas import tpu as pltpu
from jax.sharding import Mesh
from jax.sharding import PartitionSpec as P

CORES = 2
Z_GROUPS = 4
SPLIT = 4
HIDES = {"pack_b": 1e11, "pack_f": 1e11, "merge_b": 1e11}
F32 = jnp.float32
BF16 = jnp.bfloat16
VMEM = pl.BlockSpec(memory_space=pltpu.VMEM)
ANY = pl.BlockSpec(memory_space=pl.ANY)
SMEM = pl.BlockSpec(memory_space=pltpu.SMEM)
PARAMS = pltpu.CompilerParams(vmem_limit_bytes=44 * 1024 * 1024)


def iota(shape, axis):
    return lax.broadcasted_iota(jnp.int32, shape, axis)


def dot(a, b, dims=((1,), (0,))):
    return lax.dot_general(a, b, (dims, ((), ())), preferred_element_type=F32)


def ones_at(where):
    return jnp.where(where, 1.0, 0.0).astype(BF16)


def slots_of(route, experts):
    tokens = route.shape[1]
    onehot = jnp.where(iota((experts, tokens), 0) == route, 1.0, 0.0)
    shape = (tokens, tokens)
    before = dot(onehot.astype(BF16), ones_at(iota(shape, 0) < iota(shape, 1)))
    return jnp.sum(before * onehot, axis=0, keepdims=True).astype(jnp.int32)


def column(row):
    tokens = row.shape[1]
    shape = (tokens, tokens)
    on = iota(shape, 0) == iota(shape, 1)
    return jnp.sum(jnp.where(on, row, jnp.zeros((), row.dtype)), axis=1, keepdims=True)


def joined(rows, cap):
    count = rows.shape[0]
    shape = (count // 2, count)
    r, m = iota(shape, 0), iota(shape, 1)
    same = (m // (2 * cap) == r // cap) & (m % cap == r % cap)
    low = (m % (2 * cap)) // cap == 0
    parts = [dot(ones_at(same & half), rows).astype(BF16) for half in (low, ~low)]
    return jnp.concatenate(parts, axis=1)


def parted(low, high, cap, rows):
    shape = (rows, rows // 2)
    m, r = iota(shape, 0), iota(shape, 1)
    same = (m // (2 * cap) == r // cap) & (m % cap == r % cap)
    first = (m % (2 * cap)) // cap == 0
    return (dot(ones_at(same & first), low) + dot(ones_at(same & ~first), high)).astype(BF16)


def source_of(at_ref, d, block, count):
    return (at_ref[0] + count - d) % count, at_ref[1] ^ block ^ (block // 2)


def stream(far_refs, near_refs, sems):
    copies = [
        pltpu.make_async_copy(far, near, sems.at[i])
        for i, (far, near) in enumerate(zip(far_refs, near_refs))
    ]
    for copy in copies:
        copy.start()
    return copies


def slab(refs):
    return jnp.concatenate([r[...] for r in refs], axis=0)


def cut(rows, refs):
    size = rows.shape[0] // len(refs)
    for i, ref in enumerate(refs):
        ref[...] = rows[i * size : (i + 1) * size]


def pack_b_kernel(experts, cap, cot_ref, route_ref, gate_ref, out_ref):
    tokens, width = cot_ref.shape
    rows, half = out_ref.shape
    scaled = (column(gate_ref[...]) * cot_ref[...].astype(F32)).astype(BF16)
    route = route_ref[...]
    slot = slots_of(route, experts)
    m = iota((rows, tokens), 0)
    table = (m // (4 * cap) == route) & (m % cap == slot)
    low = (m % (2 * cap)) // cap == 0
    total = dot(ones_at(table & low), scaled[:, :half])
    total += dot(ones_at(table & ~low), scaled[:, half:])
    out_ref[...] = total.astype(BF16)


def expert_b_kernel(cap, c_ref, both_ref, *refs):
    far, (mine_ref, send_ref), near, sems = refs[:3], refs[3:5], refs[5:8], refs[8]
    wd_ref, saved_ref, wgu_ref = near
    wd_copy, saved_copy, wgu_copy = stream(far, near, sems)
    rows, half = mine_ref.shape
    hid, width = wd_ref.shape
    values = jnp.concatenate([joined(both_ref[:rows], cap), joined(both_ref[rows:], cap)], axis=0)
    wd_copy.wait()
    dh = dot(values, wd_ref[...], ((1,), (1,)))
    r, p = iota((rows, rows), 0), iota((rows, rows), 1)
    core = r // (rows // 2)
    r = r % (rows // 2)
    pick = (p // (2 * cap) == r // cap) & (p % cap == r % cap) & ((p % (2 * cap)) // cap == core)
    saved_copy.wait()
    saved = dot(ones_at(pick), saved_ref[...])
    act = saved[:, :hid]
    lin = saved[:, hid:]
    sig = 1.0 / (1.0 + jnp.exp(-act))
    d_act = (dh * lin * sig * (1.0 + act * (1.0 - sig))).astype(BF16)
    d_lin = (dh * act * sig).astype(BF16)
    grads = jnp.concatenate([d_act, d_lin], axis=1)
    wgu_copy.wait()
    step = 256 if half % 256 == 0 else half
    for at in range(0, half, step):
        low, high = (
            dot(grads, wgu_ref[base + at : base + at + step, :], ((1,), (1,))).astype(BF16)
            for base in (0, half)
        )
        mid = rows // 2
        first = parted(low[:mid], high[:mid], cap, rows)
        second = parted(low[mid:], high[mid:], cap, rows)
        mine_ref[:, at : at + step] = jnp.where(c_ref[0] == 0, first, second)
        send_ref[:, at : at + step] = jnp.where(c_ref[0] == 0, second, first)


def split_b_kernel(cap, at_ref, rows_ref, *out_refs):
    rows = joined(rows_ref[...], cap)
    count = rows.shape[0] // (Z_GROUPS * cap)
    shape = (rows.shape[0], rows.shape[0])
    r, m = iota(shape, 0), iota(shape, 1)
    x, z = source_of(at_ref, (r // cap) % count, r // (count * cap), count)
    pick = m == (x * Z_GROUPS + z) * cap + r % cap
    cut(dot(ones_at(pick), rows).astype(BF16), out_refs)


def merge_kernel(cap, here_ref, partner_ref, mirror_ref, opposite_ref, *out_refs):
    rows = jnp.concatenate([r[...] for r in (here_ref, partner_ref, mirror_ref, opposite_ref)], axis=0)
    shape = (len(out_refs) * 2 * cap, rows.shape[0])
    block = here_ref.shape[0]
    r, m = iota(shape, 0), iota(shape, 1)
    same = ((m % block) // cap == r // (2 * cap)) & (m % cap == r % cap)
    same = same & (m // (2 * block) == (r % (2 * cap)) // cap)
    merged = dot(ones_at(same), rows).astype(BF16)
    for d, out_ref in enumerate(out_refs):
        out_ref[...] = merged[d * 2 * cap : (d + 1) * 2 * cap]


def final_b_kernel(experts, cap, at_ref, cot_ref, route_ref, *refs):
    *in_refs, out_ref = refs
    tokens = cot_ref.shape[0]
    count = len(in_refs)
    rows = jnp.concatenate([r[...] for r in in_refs], axis=0)
    route = route_ref[...]
    slot = column(slots_of(route, experts))
    m = iota((tokens, rows.shape[0]), 1)
    pair = at_ref[1] // 2 ^ ((m % (2 * cap)) // cap)
    expert = (at_ref[0] + m // (2 * cap)) % count * 2 + pair
    total = dot(ones_at((expert == column(route)) & (m % cap == slot)), rows)
    out_ref[...] = (cot_ref[...].astype(F32) + total).astype(BF16)


def pack_f_kernel(experts, cap, at_ref, x_ref, meta_ref, *out_refs):
    tokens = x_ref.shape[0]
    route = meta_ref[0:1, :].astype(jnp.int32)
    slot = slots_of(route, experts)
    count = len(out_refs)
    m = iota((count * 2 * cap, tokens), 0)
    pair = at_ref[1] // 2 ^ ((m % (2 * cap)) // cap)
    expert = (at_ref[0] + m // (2 * cap)) % count * 2 + pair
    packed = dot(ones_at((expert == route) & (m % cap == slot)), x_ref[...]).astype(BF16)
    cut(packed, out_refs)


def pairs_kernel(cap, *refs):
    *in_refs, own_ref, oth_ref = refs
    rows = slab(in_refs)
    shape = (own_ref.shape[0], rows.shape[0])
    r, m = iota(shape, 0), iota(shape, 1)
    same = (m // (2 * cap) == r // cap) & (m % cap == r % cap)
    own = (m % (2 * cap)) // cap == 0
    own_ref[...] = dot(ones_at(same & own), rows).astype(BF16)
    oth_ref[...] = dot(ones_at(same & ~own), rows).astype(BF16)


def join_kernel(*refs):
    refs[-1][...] = slab(refs[:-1])


def expert_f_kernel(c_ref, both_ref, *refs):
    far, (mine_ref, send_ref), near, sems = refs[:2], refs[2:4], refs[4:6], refs[6]
    wgu_ref, wd_ref = near
    wgu_copy, wd_copy = stream(far, near, sems)
    rows = mine_ref.shape[0]
    hid, width = wd_ref.shape
    wgu_copy.wait()
    pre = dot(both_ref[...], wgu_ref[...])
    gate = pre[:, :hid]
    hidden = (gate / (1.0 + jnp.exp(-gate)) * pre[:, hid:]).astype(BF16)
    wd_copy.wait()
    step = 512 if width % 512 == 0 else width
    for at in range(0, width, step):
        part = dot(hidden, wd_ref[:, at : at + step]).astype(BF16)
        mine_ref[:, at : at + step] = jnp.where(c_ref[0] == 0, part[:rows], part[rows:])
        send_ref[:, at : at + step] = jnp.where(c_ref[0] == 0, part[rows:], part[:rows])


def add_kernel(a_ref, b_ref, *out_refs):
    cut((a_ref[...].astype(F32) + b_ref[...].astype(F32)).astype(BF16), out_refs)


def spread_f_kernel(cap, at_ref, *refs):
    *in_refs, out_ref = refs
    rows = slab(in_refs)
    many, half = out_ref.shape
    count = rows.shape[0] // (Z_GROUPS * cap)
    shape = (many, rows.shape[0])
    m, r = iota(shape, 0), iota(shape, 1)
    x, z = source_of(at_ref, (r // cap) % count, r // (count * cap), count)
    pick = (m // (2 * cap) == x * Z_GROUPS + z) & (m % cap == r % cap)
    low = (m % (2 * cap)) // cap == 0
    total = dot(ones_at(pick & low), rows[:, :half]) + dot(ones_at(pick & ~low), rows[:, half:])
    out_ref[...] = total.astype(BF16)


def final_f_kernel(experts, cap, x_ref, meta_ref, back_ref, out_ref):
    tokens = x_ref.shape[0]
    rows, half = back_ref.shape
    meta = meta_ref[...]
    route = meta[0:1, :].astype(jnp.int32)
    slot = column(slots_of(route, experts))
    gate = column(meta[1:2, :])
    m = iota((tokens, rows), 1)
    table = (m // (4 * cap) == column(route)) & (m % cap == slot)
    low = (m % (2 * cap)) // cap == 0
    back = back_ref[...]
    for base, part in ((0, low), (half, ~low)):
        total = gate * dot(ones_at(table & part), back)
        x = x_ref[:, base : base + half].astype(F32)
        out_ref[:, base : base + half] = (x + total).astype(BF16)


def call(kernel, name, shapes, operands, flops, earlier=(), streamed=0):
    out = [jax.ShapeDtypeStruct(s, BF16) for s in shapes]
    nbytes = sum(a.size * a.dtype.itemsize for a in (*operands, *out))
    count = len(operands)
    far = operands[count - streamed :]

    def body(*refs):
        kernel(*refs[:count], *refs[count + len(earlier) :])

    scratch = [pltpu.VMEM(a.shape, a.dtype) for a in far]
    return pl.pallas_call(
        body,
        out_shape=out,
        in_specs=[SMEM if a.ndim == 1 else VMEM for a in operands[: count - streamed]]
        + [ANY] * (streamed + len(earlier)),
        out_specs=[VMEM] * len(out),
        scratch_shapes=scratch + [pltpu.SemaphoreType.DMA((streamed,))] * (streamed > 0),
        compiler_params=PARAMS,
        name=name,
        cost_estimate=pl.CostEstimate(
            flops=flops + int(HIDES.get(name, 0)), bytes_accessed=nbytes, transcendentals=0
        ),
    )(*operands, *earlier)


def moved(block, axis, to):
    return lax.ppermute(block, axis, [(i, to(i)) for i in range(lax.axis_size(axis))])


def both_cores(block):
    return lax.all_gather(block, "c", axis=0, tiled=True)


def swap_core(block):
    return moved(block, "c", lambda i: 1 - i)


def shift(block, distance):
    count = lax.axis_size("pp")
    return moved(block, "pp", lambda i: (i + distance) % count)


def along_x(blocks, sign):
    count = len(blocks)
    rest = [moved(b, "x", lambda i, d=d: (i + sign * d) % count) for d, b in enumerate(blocks) if d]
    return [blocks[0]] + rest


def exchange(rows, cap):
    width = rows.shape[1]
    blocks = rows.reshape(-1, 2 * cap, width)
    blocks = lax.all_to_all(blocks, ("x", "zh"), split_axis=0, concat_axis=0, tiled=True)
    return blocks.reshape(-1, width)


def partner(block):
    return moved(block, "zh", lambda i: i ^ 1)


def mirror(block):
    return moved(block, "zh", lambda i: 3 - i)


def opposite(block):
    return moved(block, "zh", lambda i: i ^ 2)


def shards(fwd_in, fwd_route, fwd_gate, bwd_cot, bwd_route, bwd_gate, saved_pre, w_gate_up, w_down):
    devices = lax.axis_size(("x", "zh", "c"))
    experts = devices // SPLIT
    cap = saved_pre.shape[2] // devices
    cot = bwd_cot[0]
    tokens, width = cot.shape
    hid = w_down.shape[1]
    wgu, wd = w_gate_up[0], w_down[0]
    at = jnp.stack([lax.axis_index(a) for a in ("x", "zh", "c")]).astype(jnp.int32)
    many = devices * cap
    few = many // 2
    half = (many, width // 2)
    block = few // Z_GROUPS

    def kernel(body, *head):
        return lambda *refs: body(*head, *refs)

    route_b, gate_b = bwd_route.reshape(1, tokens), bwd_gate.reshape(1, tokens)
    x = shift(fwd_in[0], 1)
    meta = jnp.concatenate(
        [fwd_route.reshape(1, tokens).astype(F32), fwd_gate.reshape(1, tokens)], axis=0
    )
    meta = shift(meta, 1)
    core = at[2:]
    rounds = jnp.minimum(jnp.sum((bwd_route < experts).astype(jnp.int32)), 1)

    (packed,) = call(
        kernel(pack_b_kernel, experts, cap),
        "pack_b",
        [half],
        (cot, route_b, gate_b),
        2 * many * tokens * width,
    )
    own_b = exchange(packed, cap)

    chunks = call(
        kernel(pack_f_kernel, experts, cap),
        "pack_f",
        [(2 * cap, width)] * (block // cap),
        (at, x, meta),
        4 * block * tokens * width,
        earlier=(packed,),
    )
    chunks = along_x(chunks, 1)
    here, away = call(
        kernel(pairs_kernel, cap), "pairs_f", [(block, width)] * 2, chunks, 4 * block * block * width
    )
    blocks_f = (here, partner(here), mirror(away), opposite(away))

    def chain_b(_, rows):
        mine, send = call(
            kernel(expert_b_kernel, cap),
            "expert_b",
            [half] * 2,
            (core, both_cores(rows), wd, saved_pre[0, 0], wgu),
            6 * many * hid * width,
            streamed=3,
        )
        return (mine.astype(F32) + swap_core(send).astype(F32)).astype(BF16)

    summed_b = lax.fori_loop(0, rounds, chain_b, own_b)
    here, to_partner, to_mirror, to_opposite = call(
        kernel(split_b_kernel, cap),
        "split_b",
        [(block, width)] * Z_GROUPS,
        (at, summed_b),
        2 * few * many * width,
    )
    blocks_b = (here, partner(to_partner), mirror(to_mirror), opposite(to_opposite))

    def chain_f(_, blocks):
        (own,) = call(join_kernel, "join_f", [(few, width)], blocks, few * width)
        mine, send = call(
            expert_f_kernel, "expert_f", [(few, width)] * 2, (core, both_cores(own), wgu, wd), 6 * many * hid * width, streamed=2
        )
        return tuple(
            call(add_kernel, "add_f", [(block, width)] * Z_GROUPS, (mine, swap_core(send)), few * width)
        )

    summed_f = lax.fori_loop(0, rounds, chain_f, blocks_f)
    (spread,) = call(
        kernel(spread_f_kernel, cap), "spread_f", [half], (at, *summed_f), 2 * few * many * width
    )
    back_f = exchange(spread, cap)

    chunks = call(
        kernel(merge_kernel, cap),
        "merge_b",
        [(2 * cap, width)] * (block // cap),
        blocks_b,
        4 * block * few * width,
    )
    chunks = along_x(chunks, -1)
    (out_b,) = call(
        kernel(final_b_kernel, experts, cap),
        "final_b",
        [(tokens, width)],
        (at, cot, route_b, *chunks),
        4 * block * tokens * width,
    )
    out_b = shift(out_b, -1)
    (out_f,) = call(
        kernel(final_f_kernel, experts, cap),
        "final_f",
        [(tokens, width)],
        (x, meta, back_f),
        2 * many * tokens * width,
    )
    return out_f[None], out_b[None]


def solution(mesh):
    sections, members = mesh.devices.shape
    fine = Mesh(
        mesh.devices.reshape(sections, members // (Z_GROUPS * CORES), Z_GROUPS, CORES),
        ("pp", "x", "zh", "c"),
    )
    ep = ("x", "zh", "c")
    rows = P("pp", ep, None)
    return jax.shard_map(
        shards,
        mesh=fine,
        in_specs=(rows,) * 6 + (P("pp", ep, None, None), P(ep, None, None), P(ep, None, None)),
        out_specs=(rows, rows),
        check_vma=False,
    )
```
